32 devices in a mesh: member: 2 (over y), lat: 4 (over x, core), lon: 4 (over z).
Axes of the slice: x: 2, y: 2, z: 4, core: 2. Of those that a mesh axis runs over, the one named last changes fastest.
Arguments:
- fields: float32 [4, 192, 32, 512], P('member', None, 'lat', 'lon'), parts along dimension 0, may hold values from -6 to 6
- wind_east: float32 [32, 512], P('lat', 'lon'), may hold values from -0.3 to 0.3
- wind_north: float32 [32, 512], P('lat', 'lon'), may hold values from -0.3 to 0.3
- diffusion: float32 [32, 512], P('lat', 'lon'), may hold values from 0.01 to 0.08
- inflow_owner: int32 [256, 1], P(('lat', 'lon')), may hold values from 0 to 3; in each aligned block of 16 rows (0 to 15, 16 to 31, ...) at most 8 rows name the same one
- inflow_cell: int32 [256, 128], P(('lat', 'lon')), may hold values from 0 to 1023
- inflow_node: int32 [256, 128], P(('lat', 'lon')), may hold values from 0 to 255
- inflow_weight: float32 [256, 128], P(('lat', 'lon')), may hold values from 0.25 to 1.5
- encoder: bfloat16 [192, 512], replicated, may hold values from -0.21875 to 0.21875
- sender_weight: bfloat16 [2, 512, 512], replicated, may hold values from -0.25 to 0.25
- receiver_weight: bfloat16 [2, 512, 512], replicated, may hold values from -0.25 to 0.25
- update_weight: bfloat16 [2, 512, 512], replicated, may hold values from -0.25 to 0.25
- decoder: bfloat16 [512, 192], replicated, may hold values from -0.25 to 0.25
- edge_sender: int32 [4, 4, 1536], P('lat', 'lon'), may hold values from 0 to 447, as said below
- edge_receiver: int32 [4, 4, 1536], P('lat', 'lon'), may hold values from 0 to 255
- halo_rows: int32 [4, 4, 4, 48], P('lat', 'lon'), may hold values from 0 to 255
- outflow_owner: int32 [256, 1], P(('lat', 'lon')), may hold values from 0 to 3; in each aligned block of 16 rows (0 to 15, 16 to 31, ...) at most 8 rows name the same one
- outflow_node: int32 [256, 128], P(('lat', 'lon')), may hold values from 0 to 255
- outflow_cell: int32 [256, 128], P(('lat', 'lon')), may hold values from 0 to 1023
- outflow_weight: float32 [256, 128], P(('lat', 'lon')), may hold values from 0.25 to 1.5
Outputs:
- revised_outlook: float32 [4, 192, 32, 512], P('member', None, 'lat', 'lon'), parts along dimension 0
The draws below stay inside these ranges and needn't reach their ends.
There are 2 independent parts, one for each index of `member`. The reference program is written for one: setup_inputs(seed, part) draws one part's arguments, and reference() takes and returns one part's arrays. A program takes and returns all parts, laid end to end along the dimension named above; an argument that names none is the same for every part. Nothing has to cross between parts.
Inputs may be any that keep to these rules, and one draw needn't show every extreme that they name: `inflow_owner`: among the 16 rows of one device, no lon index appears more than 8 times. `outflow_owner`: among the 16 rows of one device, no lon index appears more than 8 times. `edge_sender`: A value below 256 names a node of the edge's own partition; a value 256 + q * 48 + p names halo slot p toward neighbour q as in the reference program. No edge of the first lat index uses q = 0, none of the last uses q = 1.
All inputs are finite; a program needn't handle non-finite values.
Results may differ from the reference program's by a relative error of at most 0.0075.
Values may be sent and summed in bfloat16 or wider, within the bound.
No kernel may reach another device: no remote copies, remote signals or barrier semaphores. Data moves between devices by JAX's collectives and lax.ppermute only.
A program may use at most 128 MiB of HBM per device.

```python
import math
import jax
import jax.numpy as jnp
import numpy as np
from jax import lax

BATCH_REALIZATION = 2
POINT_QUANTITIES = 192
PATCH_PARALLELS = 8
PATCH_MERIDIANS = 128
GLOBE_PARALLELS = 32
GLOBE_MERIDIANS = 512
DSTEPS = 2
BLOCKS = 16
ENTRIES = 128
CAP = 8
ROWS = 256
NODE_DEV = 256
NODES = 4096
HCAP = 48
EDGES = 1536
HID = 512
LAYERS = 2
N_LAT = 4
N_LON = 4


def draw_edge_sender(key, part):
    base = jax.random.fold_in(key, 41)
    keys = jax.random.split(base, 4)
    shape = (N_LAT, N_LON, EDGES)
    choose_local = jax.random.randint(keys[0], shape, 0, 10)
    local_node = jax.random.randint(keys[1], shape, 0, NODE_DEV)
    quarter = jax.random.randint(keys[2], shape, 0, 4)
    lat_index = jnp.arange(N_LAT, dtype=jnp.int32)[:, None, None]
    missing = (quarter == 0) & (lat_index == 0) | (quarter == 1) & (lat_index == N_LAT - 1)
    quarter = jnp.where(missing, quarter + 2, quarter)
    slot_index = jax.random.randint(keys[3], shape, 0, HCAP)
    result = jnp.where(choose_local < 6, local_node, NODE_DEV + quarter * HCAP + slot_index)
    return result.astype(jnp.int32)


def touch_ends(values, rng, low, high):
    index_at = [jax.random.randint(jax.random.fold_in(rng, axis), (), 0, length) for axis, length in enumerate(values.shape)]
    longest = values.shape.index(max(values.shape))
    neighbour = index_at[:longest] + [(index_at[longest] + 1) % values.shape[longest]] + index_at[longest + 1:]
    return values.at[tuple(index_at)].set(low).at[tuple(neighbour)].set(high)


def shard_levels(rng, extent, pieces, least, high):
    level, own = 1.0, jax.random.fold_in(rng, 6)
    for position, parts in pieces:
        steps = jnp.exp(jax.random.uniform(jax.random.fold_in(own, position), (parts,), jnp.float32, least / len(pieces), high / len(pieces)))
        level = level * jnp.repeat(steps, extent[position] // parts).reshape([-1 if axis == position else 1 for axis in range(len(extent))])
    return level


def shared_out(stream_key, own, number, rows, number_of, top, limit, skew):
    sequence = jax.random.permutation(stream_key, number_of)
    heavy_load, ordinary = load_shares(number_of, rows * top, limit, skew, True), load_shares(number_of, rows * top, limit, skew, False)
    places = jnp.arange(number_of)

    def named(sizes, offset_by):
        used = int((sizes > 0).sum())
        fixed = max(1, used // 4)
        passed = fixed + (places - fixed + offset_by * (used - fixed)) % max(1, number_of - fixed)
        return jnp.zeros((number_of,), jnp.int32).at[sequence[jnp.where(places < fixed, places, passed)]].set(jnp.asarray(sizes, jnp.int32))

    sizes = jnp.where(number % 4 == 0, named(heavy_load, number // 4), named(ordinary, number - number // 4 - 1))
    mixed = jax.random.permutation(jax.random.fold_in(own, 3), number_of)
    source_of, sink = mixed[0:number_of // 2 * 2:2], mixed[1:number_of // 2 * 2:2]
    margin = jnp.minimum(sizes[source_of] - 1, limit - sizes[sink]) // 2
    margin = jnp.where((source_of == sequence[0]) | (sink == sequence[0]) | (sizes[sink] == 0), 0, jnp.maximum(margin, 0))
    passed = jax.random.randint(jax.random.fold_in(own, 4), (number_of // 2,), 0, 1 << 20) % (margin + 1)
    sizes = sizes.at[source_of].add(-passed).at[sink].add(passed)
    labels = jnp.searchsorted(jnp.cumsum(sizes), jnp.arange(rows * top), side="right").astype(jnp.int32)
    grid = labels.reshape(top, rows).T
    grid = grid[jax.random.permutation(jax.random.fold_in(own, 1), rows)]
    offset_by = jax.random.randint(jax.random.fold_in(own, 2), (rows, 1), 0, top)
    return jnp.take_along_axis(grid, (jnp.arange(top)[None, :] + offset_by) % top, axis=1)


def load_shares(amount, total, limit, skew, full):
    loads = [(1 << 20) // math.isqrt(standing ** skew) + 1 for standing in range(1, amount + 1)]
    largest = limit if full else min(limit, max(-(-total // amount), total * loads[0] // sum(loads)))
    least = 1 if total - largest >= amount - 1 else 0
    counts, rest = [largest] + [least] * (amount - 1), total - largest - least * (amount - 1)
    while rest > 0:
        movable = [i for i in range(1, amount) if counts[i] < largest] or [i for i in range(1, amount) if counts[i] < limit]
        mass, budget = sum([loads[i] for i in movable]), rest
        for i in movable:
            extra = min(limit - counts[i], max(1, budget * loads[i] // mass), rest)
            counts[i] = counts[i] + extra
            rest = rest - extra
    return np.array(counts)


def noise(own_key, dims, scale, bound, pieces=(), kind=jnp.bfloat16):
    values = scale * jax.random.normal(own_key, dims, jnp.float32)
    if pieces:
        values = values * shard_levels(own_key, dims, pieces, -0.22, 0.18)
    return jnp.clip(values, -bound, bound).astype(kind)


def setup_inputs(seed: int = 0, part: int = 0) -> dict:
    key_of = jax.random.split(jax.random.key(seed), 21)
    part_keys = jax.random.split(jax.random.fold_in(key_of[20], part), 21)
    fields = noise(part_keys[0], (BATCH_REALIZATION, POINT_QUANTITIES, GLOBE_PARALLELS, GLOBE_MERIDIANS), 1.0, 6.0, ((2, 4), (3, 4)), jnp.float32)
    wind_east = jnp.clip(jax.random.uniform(key_of[1], (GLOBE_PARALLELS, GLOBE_MERIDIANS), jnp.float32, -0.3, 0.3) * shard_levels(key_of[1], (GLOBE_PARALLELS, GLOBE_MERIDIANS), ((0, 4), (1, 4)), -0.4, 0.0), -0.3, 0.3)
    wind_north = jnp.clip(jax.random.uniform(key_of[2], (GLOBE_PARALLELS, GLOBE_MERIDIANS), jnp.float32, -0.3, 0.3) * shard_levels(key_of[2], (GLOBE_PARALLELS, GLOBE_MERIDIANS), ((0, 4), (1, 4)), -0.4, 0.0), -0.3, 0.3)
    diffusion = jnp.clip(jnp.exp(math.log(0.08) - 2.0794415 * jax.random.uniform(key_of[3], (GLOBE_PARALLELS, GLOBE_MERIDIANS), jnp.float32) ** shard_levels(key_of[3], (GLOBE_PARALLELS, GLOBE_MERIDIANS), ((0, 4), (1, 4)), -0.2, 0.2)), 0.01, 0.08)
    inflow_owner_keys = jax.random.split(jax.random.fold_in(key_of[4], 1), ROWS // BLOCKS)
    inflow_owner_turns = jax.random.permutation(jax.random.fold_in(key_of[4], 3), ROWS // BLOCKS)
    inflow_owner = jax.vmap(lambda own, number: shared_out(jax.random.fold_in(key_of[4], 2), own, number, BLOCKS, N_LON, 1, CAP, 2))(inflow_owner_keys, inflow_owner_turns).reshape((ROWS, 1))
    inflow_cell = touch_ends(jax.random.randint(key_of[5], (ROWS, ENTRIES), 0, PATCH_PARALLELS * PATCH_MERIDIANS), jax.random.fold_in(key_of[5], 1), 0, (PATCH_PARALLELS * PATCH_MERIDIANS) - 1).astype(jnp.int32)
    inflow_node = touch_ends(jax.random.randint(key_of[6], (ROWS, ENTRIES), 0, NODE_DEV), jax.random.fold_in(key_of[6], 1), 0, NODE_DEV - 1).astype(jnp.int32)
    inflow_weight = jnp.clip(0.25 + 1.25 * jax.random.uniform(key_of[7], (ROWS, ENTRIES), jnp.float32) ** shard_levels(key_of[7], (ROWS, ENTRIES), ((0, 16),), -0.2, 0.2), 0.25, 1.5)
    encoder = noise(key_of[8], (POINT_QUANTITIES, HID), (4 * POINT_QUANTITIES) ** -0.5, 0.21875)
    sender_weight = noise(key_of[9], (LAYERS, HID, HID), HID ** -0.5, 0.25)
    receiver_weight = noise(key_of[10], (LAYERS, HID, HID), HID ** -0.5, 0.25)
    update_weight = noise(key_of[11], (LAYERS, HID, HID), HID ** -0.5, 0.25)
    decoder = noise(key_of[12], (HID, POINT_QUANTITIES), HID ** -0.5, 0.25)
    edge_sender = draw_edge_sender(jax.random.fold_in(key_of[20], 71), part)
    edge_receiver = touch_ends(jax.random.randint(key_of[14], (N_LAT, N_LON, EDGES), 0, NODE_DEV), jax.random.fold_in(key_of[14], 1), 0, NODE_DEV - 1).astype(jnp.int32)
    halo_rows = touch_ends(jax.random.randint(key_of[15], (N_LAT, N_LON, 4, HCAP), 0, NODE_DEV), jax.random.fold_in(key_of[15], 1), 0, NODE_DEV - 1).astype(jnp.int32)
    outflow_owner_keys = jax.random.split(jax.random.fold_in(key_of[16], 1), ROWS // BLOCKS)
    outflow_owner_turns = jax.random.permutation(jax.random.fold_in(key_of[16], 3), ROWS // BLOCKS)
    outflow_owner = jax.vmap(lambda own, number: shared_out(jax.random.fold_in(key_of[16], 2), own, number, BLOCKS, N_LON, 1, CAP, 2))(outflow_owner_keys, outflow_owner_turns).reshape((ROWS, 1))
    outflow_node = touch_ends(jax.random.randint(key_of[17], (ROWS, ENTRIES), 0, NODE_DEV), jax.random.fold_in(key_of[17], 1), 0, NODE_DEV - 1).astype(jnp.int32)
    outflow_cell = touch_ends(jax.random.randint(key_of[18], (ROWS, ENTRIES), 0, PATCH_PARALLELS * PATCH_MERIDIANS), jax.random.fold_in(key_of[18], 1), 0, (PATCH_PARALLELS * PATCH_MERIDIANS) - 1).astype(jnp.int32)
    outflow_weight = jnp.clip(0.25 + 1.25 * jax.random.uniform(key_of[19], (ROWS, ENTRIES), jnp.float32) ** shard_levels(key_of[19], (ROWS, ENTRIES), ((0, 16),), -0.2, 0.2), 0.25, 1.5)
    return dict(fields=fields, wind_east=wind_east, wind_north=wind_north, diffusion=diffusion, inflow_owner=inflow_owner, inflow_cell=inflow_cell, inflow_node=inflow_node, inflow_weight=inflow_weight, encoder=encoder, sender_weight=sender_weight, receiver_weight=receiver_weight, update_weight=update_weight, decoder=decoder, edge_sender=edge_sender, edge_receiver=edge_receiver, halo_rows=halo_rows, outflow_owner=outflow_owner, outflow_node=outflow_node, outflow_cell=outflow_cell, outflow_weight=outflow_weight)


def advance(extended, east_rate, north_rate, spread):
    middle = extended[:, 1:-1, 1:-1]
    west_cells = extended[:, 1:-1, :-2]
    east_cells = extended[:, 1:-1, 2:]
    south_cells = extended[:, :-2, 1:-1]
    north_cells = extended[:, 2:, 1:-1]
    result = middle - jnp.maximum(east_rate, 0.0) * (middle - west_cells)
    result = result - jnp.minimum(east_rate, 0.0) * (east_cells - middle)
    result = result - jnp.maximum(north_rate, 0.0) * (middle - south_cells)
    result = result - jnp.minimum(north_rate, 0.0) * (north_cells - middle)
    return result + spread * (west_cells + east_cells + south_cells + north_cells - 4.0 * middle)

def normalize(values):
    scale = lax.rsqrt(lax.optimization_barrier(jnp.mean(values * values, axis=-1, keepdims=True)) + 1e-06)
    return (values * scale).astype(jnp.bfloat16)

def reference(fields, wind_east, wind_north, diffusion, inflow_owner, inflow_cell, inflow_node, inflow_weight, encoder, sender_weight, receiver_weight, update_weight, decoder, edge_sender, edge_receiver, halo_rows, outflow_owner, outflow_node, outflow_cell, outflow_weight):
    latent_quantities = BATCH_REALIZATION * POINT_QUANTITIES
    current_condition = fields.reshape(latent_quantities, GLOBE_PARALLELS, GLOBE_MERIDIANS)
    for sub_step in range(DSTEPS):
        extended = jnp.pad(current_condition, ((0, 0), (1, 1), (0, 0)), mode='edge')
        extended = jnp.concatenate([extended[:, :, -1:], extended, extended[:, :, :1]], axis=2)
        current_condition = advance(extended, wind_east, wind_north, diffusion)
    device_count = N_LAT * N_LON
    block_rows = inflow_owner.shape[0]
    device_of = jnp.arange(block_rows, dtype=jnp.int32) // BLOCKS
    lat_of = (device_of // N_LON)[:, None]
    lon_of = (device_of % N_LON)[:, None]
    table = current_condition.reshape(latent_quantities, GLOBE_PARALLELS * GLOBE_MERIDIANS).T
    grid_index = (lat_of * PATCH_PARALLELS + inflow_cell // PATCH_MERIDIANS) * GLOBE_MERIDIANS + lon_of * PATCH_MERIDIANS + inflow_cell % PATCH_MERIDIANS
    inflow = (jnp.take(table, grid_index.reshape(-1).astype(jnp.int32), axis=0) * inflow_weight.reshape(-1, 1)).astype(jnp.bfloat16)
    node_index = ((lat_of * N_LON + inflow_owner) * NODE_DEV + inflow_node).reshape(-1).astype(jnp.int32)
    node_input = jax.ops.segment_sum(inflow.astype(jnp.float32), node_index, num_segments=NODES)
    embedded = node_input.astype(jnp.bfloat16).reshape(NODES * BATCH_REALIZATION, POINT_QUANTITIES)
    hidden = jax.nn.silu(jnp.dot(embedded, encoder, preferred_element_type=jnp.float32))
    lat_step = jnp.array([-1, 1, 0, 0], dtype=jnp.int32)
    lon_step = jnp.array([0, 0, -1, 1], dtype=jnp.int32)
    lat_grid = jnp.arange(N_LAT, dtype=jnp.int32)[:, None, None]
    lon_grid = jnp.arange(N_LON, dtype=jnp.int32)[None, :, None]
    device_grid = lat_grid * N_LON + lon_grid
    is_local = edge_sender < NODE_DEV
    relative = jnp.maximum(edge_sender - NODE_DEV, 0)
    quarter = jnp.clip(relative // HCAP, 0, 3)
    slot_index = relative % HCAP
    near_lat = jnp.clip(lat_grid + lat_step[quarter], 0, N_LAT - 1)
    near_lon = (lon_grid + lon_step[quarter]) % N_LON
    halo_flat = halo_rows.reshape(N_LAT, N_LON, 4 * HCAP)
    halo_node = jnp.take_along_axis(halo_flat, jnp.where(is_local, 0, quarter * HCAP + slot_index).astype(jnp.int32), axis=2)
    sender_global = jnp.where(is_local, device_grid * NODE_DEV + edge_sender, (near_lat * N_LON + near_lon) * NODE_DEV + halo_node)
    sender_global = sender_global.reshape(device_count, EDGES).astype(jnp.int32)
    receiver_local = edge_receiver.reshape(device_count, EDGES).astype(jnp.int32)
    device_ids = jnp.arange(device_count, dtype=jnp.int32)
    for layer in range(LAYERS):
        normed = normalize(hidden)
        source = jnp.dot(normed, sender_weight[layer], preferred_element_type=jnp.float32).astype(jnp.bfloat16).reshape(NODES, BATCH_REALIZATION, HID)
        target = jnp.dot(normed, receiver_weight[layer], preferred_element_type=jnp.float32).reshape(NODES, BATCH_REALIZATION, HID)

        def partition(operands):
            senders, receivers, device = operands
            own_target = lax.dynamic_slice_in_dim(target, (device * NODE_DEV).astype(jnp.int32), NODE_DEV, 0)
            summed = jnp.take(source, senders, axis=0).astype(jnp.float32) + jnp.take(own_target, receivers, axis=0)
            message = jax.nn.silu(summed).astype(jnp.bfloat16)
            return jax.ops.segment_sum(message.astype(jnp.float32), receivers, num_segments=NODE_DEV).astype(jnp.bfloat16)
        collected = lax.map(partition, (sender_global, receiver_local, device_ids))
        collected = collected.reshape(NODES * BATCH_REALIZATION, HID)
        hidden = hidden + jnp.dot(collected, update_weight[layer], preferred_element_type=jnp.float32)
    correction = jnp.dot(normalize(hidden), decoder, preferred_element_type=jnp.float32).astype(jnp.bfloat16).reshape(NODES, latent_quantities)
    source_node = (device_of[:, None] * NODE_DEV + outflow_node).reshape(-1).astype(jnp.int32)
    outflow = (jnp.take(correction, source_node, axis=0).astype(jnp.float32) * outflow_weight.reshape(-1, 1)).astype(jnp.bfloat16)
    cell_index = (lat_of * PATCH_PARALLELS + outflow_cell // PATCH_MERIDIANS) * GLOBE_MERIDIANS + outflow_owner * PATCH_MERIDIANS + outflow_cell % PATCH_MERIDIANS
    add_learned_fix = jax.ops.segment_sum(outflow.astype(jnp.float32), cell_index.reshape(-1).astype(jnp.int32), num_segments=GLOBE_PARALLELS * GLOBE_MERIDIANS)
    revised_outlook = current_condition + add_learned_fix.T.reshape(latent_quantities, GLOBE_PARALLELS, GLOBE_MERIDIANS)
    return revised_outlook.reshape(BATCH_REALIZATION, POINT_QUANTITIES, GLOBE_PARALLELS, GLOBE_MERIDIANS)
```

```python
import functools

import jax
import jax.numpy as jnp
from jax import lax
from jax.experimental import pallas as pl
from jax.experimental.pallas import tpu as pltpu
from jax.sharding import PartitionSpec as P

F32, BF16, I32 = jnp.float32, jnp.bfloat16, jnp.int32
MIB = 1 << 20
NODE_DEV = 256


def dot(a, b, ca=1, cb=0):
    return lax.dot_general(a, b, (((ca,), (cb,)), ((), ())), preferred_element_type=F32)


def iota(shape, dim):
    return lax.broadcasted_iota(I32, shape, dim)


def call(kernel, outs, args, smem=0, scratch=(), vmem=32, cost=None):
    spaces = [pltpu.SMEM] * smem + [pltpu.VMEM] * (len(args) - smem)
    single = not isinstance(outs, (list, tuple))
    out = pl.pallas_call(
        kernel,
        out_shape=outs if single else tuple(outs),
        in_specs=[pl.BlockSpec(memory_space=s) for s in spaces],
        out_specs=pl.BlockSpec(memory_space=pltpu.VMEM)
        if single
        else tuple(pl.BlockSpec(memory_space=pltpu.VMEM) for _ in outs),
        scratch_shapes=list(scratch),
        compiler_params=pltpu.CompilerParams(vmem_limit_bytes=vmem * MIB),
        cost_estimate=cost,
    )(*args)
    return out


def cost(flops, bytes_accessed):
    return pl.CostEstimate(flops=int(flops), bytes_accessed=int(bytes_accessed), transcendentals=0)


def shape(dims, dtype):
    return jax.ShapeDtypeStruct(tuple(dims), dtype)


def split(v):
    hi = v.astype(BF16).astype(F32)
    return hi, v - hi


def pick_columns(width):
    row, lane = iota((16, width), 0), iota((16, width), 1)
    hit = (row == 0) & (lane == 0) | (row == 1) & (lane == 1)
    hit = hit | (row == 2) & (lane == width - 1) | (row == 3) & (lane == width - 2)
    return hit.astype(F32).astype(BF16)


def coefficients(we, wn, d):
    pe, ne = jnp.maximum(we, 0.0), jnp.minimum(we, 0.0)
    pn, nn = jnp.maximum(wn, 0.0), jnp.minimum(wn, 0.0)
    return 1.0 - pe + ne - pn + nn - 4.0 * d, pe + d, d - ne, pn + d, d - nn


def edge_kernel(rows, wanted, x_ref, we_ref, wn_ref, d_ref, halo_ref, up_ref, down_ref, col_ref):
    count = x_ref.shape[0] // rows
    width = x_ref.shape[1]

    def row(r):
        return x_ref[pl.ds(r, count, stride=rows), :].astype(BF16)

    line = iota((16, width), 0)
    for out_ref, near, far, q in ((up_ref, rows - 1, rows - 2, 1), (down_ref, 0, 1, 0)):
        out_ref[0:count, :] = row(near)
        out_ref[count : 2 * count, :] = row(far)
        block = jnp.zeros((16, width), F32)
        for j, ref in enumerate((we_ref, wn_ref, d_ref)):
            hi, lo = split(ref[near : near + 1, :])
            block = jnp.where(line == j, hi, jnp.where(line == j + 3, lo, block))
        out_ref[2 * count : 2 * count + 16, :] = block.astype(BF16)
        out_ref[2 * count + 16 : 2 * count + 16 + wanted, :] = jnp.broadcast_to(
            halo_ref[q * wanted : (q + 1) * wanted, :].astype(F32), (wanted, width)
        ).astype(BF16)
    pick = pick_columns(width)
    for r in range(rows):
        got = dot(pick, row(r), 1, 1)
        for k in range(4):
            col_ref[k * rows + r : k * rows + r + 1, :] = got[k : k + 1, :]


def side_kernel(rows, wanted, south_ref, north_ref, col_ref, we_ref, wn_ref, d_ref, halo_ref, east_ref, west_ref):
    count = col_ref.shape[1]
    width = we_ref.shape[1]
    pick = pick_columns(width)
    south = dot(pick, south_ref[0:count, :], 1, 1)
    north = dot(pick, north_ref[0:count, :], 1, 1)
    line, lane = iota((rows, count), 0), iota((rows, count), 1)
    for out_ref, k, c, q in ((east_ref, 2, width - 1, 3), (west_ref, 0, 0, 2)):
        corner = jnp.where(line == 0, south[k : k + 1, :], jnp.where(line == 1, north[k : k + 1, :], 0.0))
        rates = jnp.zeros((rows, count), F32)
        for j, ref in enumerate((we_ref, wn_ref, d_ref)):
            hi, lo = split(ref[:, c : c + 1])
            rates = jnp.where(lane == j, hi, jnp.where(lane == j + 3, lo, rates))
        body = [col_ref[k * rows : (k + 2) * rows, :], corner, rates]
        out_ref[0 : 4 * rows, :] = jnp.concatenate(body, 0).astype(BF16)
        out_ref[4 * rows : 4 * rows + wanted, :] = jnp.broadcast_to(
            halo_ref[q * wanted : (q + 1) * wanted, :].astype(F32), (wanted, count)
        ).astype(BF16)


def build_kernel(by_owner, slots, per, me_ref, owner_ref, node_ref, cell_ref, weight_ref, out_ref, acc):
    nodes, cells = acc.shape[1], acc.shape[2]
    entries = node_ref.shape[1]
    acc[...] = jnp.zeros(acc.shape, F32)

    @pl.loop(0, node_ref.shape[0])
    def _(b):
        if by_owner:
            slot = lax.rem(owner_ref[b] - me_ref[0] + slots, slots)
            mine = True
        else:
            slot = b // per
            mine = owner_ref[b] == me_ref[0]

        @pl.when(mine)
        def _():
            node = node_ref[pl.ds(b, 1), :].astype(I32)
            cell = cell_ref[pl.ds(b, 1), :].astype(I32)
            hot = jnp.where(iota((nodes, entries), 0) == node, 1.0, 0.0).astype(BF16)
            spread = jnp.where(iota((cells, entries), 0) == cell, weight_ref[pl.ds(b, 1), :], 0.0).astype(BF16)
            acc[slot] += dot(hot, spread, 1, 1)

    for s in range(slots):
        out_ref[s] = acc[s].astype(BF16)


def build(by_owner, slots, nodes, cells, per, me, owner, node, cell, weight):
    size = slots * nodes * cells
    return call(
        functools.partial(build_kernel, by_owner, slots, per),
        shape((slots, nodes, cells), BF16),
        (me, owner, node, cell, weight),
        smem=2,
        scratch=[pltpu.VMEM((slots, nodes, cells), F32)],
        vmem=8 + 8 * size // MIB,
        cost=cost(2 * 16 * node.shape[1] * nodes * cells, 4 * size),
    )


def step_kernel(
    rows, slots, nodes,
    x_ref, we_ref, wn_ref, d_ref, col_ref, south_ref, north_ref, west_ref, east_ref, pole_ref, a_ref,
    u_ref, *rest,
):
    part_refs, (b1, b2, keys, flat) = rest[:slots], rest[slots:]
    count = x_ref.shape[0] // rows
    width = x_ref.shape[1]
    at_south, at_north = pole_ref[0:1, 0:1], pole_ref[1:2, 0:1]

    sel_row, sel_lane = iota((8, width), 0), iota((8, width), 1)
    select = (sel_row % 2 == 0) & (sel_row < 4) & (sel_lane == 0)
    select = select | (sel_row % 2 == 1) & (sel_row < 4) & (sel_lane == width - 1)
    select = jnp.where(select, 1.0, 0.0).astype(BF16)
    key_line = iota((8, count), 0)

    def place(west, east):
        wh, wl = split(west)
        eh, el = split(east)
        key = jnp.where(key_line == 0, wh, jnp.where(key_line == 1, eh, 0.0))
        key = jnp.where(key_line == 2, wl, jnp.where(key_line == 3, el, key))
        return dot(key.astype(BF16), select, 0, 0)

    c0, cw, ce, cs, cn = coefficients(we_ref[...], wn_ref[...], d_ref[...])
    line, lane = iota((rows, width), 0), iota((rows, width), 1)
    c0 = c0 + jnp.where(line == 0, at_south * cs, 0.0) + jnp.where(line == rows - 1, at_north * cn, 0.0)
    edge_w, edge_e = cw[:, 0:1], ce[:, width - 1 : width]
    edge_s, edge_n = cs[0:1, :] * (1.0 - at_south), cn[rows - 1 : rows, :] * (1.0 - at_north)
    cw = jnp.where(lane == 0, 0.0, cw)
    ce = jnp.where(lane == width - 1, 0.0, ce)
    cs = jnp.where(line == 0, 0.0, cs)
    cn = jnp.where(line == rows - 1, 0.0, cn)

    def boundary(b_ref, west, east, south, north):
        bw, be = edge_w * west, edge_e * east
        for r in range(rows):
            placed = place(bw[r : r + 1, :], be[r : r + 1, :])
            if r == 0:
                placed = placed + edge_s * south
            if r == rows - 1:
                placed = placed + edge_n * north
            b_ref[pl.ds(r, count, stride=rows), :] = placed

    s1, s2 = south_ref[0:count, :].astype(F32), south_ref[count : 2 * count, :].astype(F32)
    n1, n2 = north_ref[0:count, :].astype(F32), north_ref[count : 2 * count, :].astype(F32)
    west, east = west_ref[...].astype(F32), east_ref[...].astype(F32)
    w1, w2, w_corner, w_rate = (west[k * rows : (k + 1) * rows, :] for k in range(4))
    e1, e2, e_corner, e_rate = (east[k * rows : (k + 1) * rows, :] for k in range(4))
    boundary(b1, w1, e1, s1, n1)

    full = iota((count, width), 1)

    def ring_row(rate_ref, at, mid, south, north):
        rate = rate_ref[2 * count : 2 * count + 16, :].astype(F32)
        k0, kw, ke, ks, kn = coefficients(*(rate[j : j + 1, :] + rate[j + 3 : j + 4, :] for j in range(3)))
        ends = place(w_corner[at : at + 1, :], e_corner[at : at + 1, :])
        to_w = jnp.where(full == 0, ends, pltpu.roll(mid, 1, 1))
        to_e = jnp.where(full == width - 1, ends, pltpu.roll(mid, width - 1, 1))
        return k0 * mid + kw * to_w + ke * to_e + ks * south + kn * north

    def ring_col(rate, corner, mid, out_w, out_e):
        k0, kw, ke, ks, kn = coefficients(*(rate[:, j : j + 1] + rate[:, j + 3 : j + 4] for j in range(3)))
        first = iota(k0.shape, 0)
        k0 = k0 + jnp.where(first == 0, at_south * ks, 0.0) + jnp.where(first == rows - 1, at_north * kn, 0.0)
        ks = ks * jnp.where(first == 0, 1.0 - at_south, 1.0)
        kn = kn * jnp.where(first == rows - 1, 1.0 - at_north, 1.0)
        step = iota(mid.shape, 0)
        to_s = jnp.where(step == 0, corner[0:1, :], pltpu.roll(mid, 1, 0))
        to_n = jnp.where(step == rows - 1, corner[1:2, :], pltpu.roll(mid, rows - 1, 0))
        return k0 * mid + kw * out_w + ke * out_e + ks * to_s + kn * to_n

    ring_s = ring_row(south_ref, 0, s1, s2, x_ref[pl.ds(0, count, stride=rows), :])
    ring_n = ring_row(north_ref, 1, n1, x_ref[pl.ds(rows - 1, count, stride=rows), :], n2)
    ring_w = ring_col(w_rate, w_corner, w1, w2, col_ref[0:rows, :])
    ring_e = ring_col(e_rate, e_corner, e1, col_ref[2 * rows : 3 * rows, :], e2)
    boundary(b2, ring_w, ring_e, ring_s, ring_n)

    group = 8

    @pl.loop(0, count // group)
    def _(g):
        here = pl.ds(pl.multiple_of(g * group * rows, group * rows), group * rows)

        def step(v, b_ref):
            v = c0 * v + cw * pltpu.roll(v, 1, 2) + ce * pltpu.roll(v, width - 1, 2) + (
                cs * pltpu.roll(v, 1, 1) + cn * pltpu.roll(v, rows - 1, 1)
            )
            return v + b_ref[here, :].reshape(group, rows, width)

        v = step(step(x_ref[here, :].reshape(group, rows, width), b1), b2)
        u_ref[here, :] = v.reshape(group * rows, width)

    for r in range(rows):
        flat[:, r * width : (r + 1) * width] = u_ref[pl.ds(r, count, stride=rows), :].astype(BF16)
    for s in range(slots):
        part_refs[s][...] = dot(a_ref[s], flat[...], 1, 1).astype(part_refs[s].dtype)


def silu(v):
    return 0.5 * v * (1.0 + jnp.tanh(0.5 * v))


def normalize(v):
    return (v * lax.rsqrt(jnp.mean(v * v, axis=-1, keepdims=True) + 1e-06)).astype(BF16)


def link_kernel(sender_ref, receiver_ref, row_ref, gather_ref, scatter_ref):
    edges, known = gather_ref.shape
    nodes = scatter_ref.shape[0]
    lane = iota((edges, nodes), 1)
    gather_ref[:, 0:nodes] = jnp.where(sender_ref[...] == lane, 1.0, 0.0).astype(BF16)
    gather_ref[:, nodes : 2 * nodes] = jnp.where(receiver_ref[...] == lane, 1.0, 0.0).astype(BF16)
    rest = iota((edges, known - 2 * nodes), 1) + nodes
    gather_ref[:, 2 * nodes :] = jnp.where(sender_ref[...] == rest, 1.0, 0.0).astype(BF16)
    scatter_ref[...] = jnp.where(row_ref[...] == iota((nodes, edges), 0), 1.0, 0.0).astype(BF16)


def project(m, hidden, owed, ws, wr, table_ref, out_refs, wanted, nodes):
    normed = normalize(hidden)
    source = dot(normed, ws).astype(BF16)
    table_ref[m, 0:nodes, :] = source
    table_ref[m, nodes : 2 * nodes, :] = dot(normed, wr).astype(BF16)
    for q in range(4):
        out_refs[q][m * wanted : (m + 1) * wanted, :] = dot(owed[q], source).astype(BF16)


def encode_kernel(
    slots, rows, count, wanted,
    *refs,
):
    part_refs = refs[:slots]
    enc_ref, ws_ref, wr_ref, south_ref, north_ref, west_ref, east_ref = refs[slots : slots + 7]
    hidden_ref, table_ref, owed_ref, *out_refs, pad = refs[slots + 7 :]
    nodes = part_refs[0].shape[0]
    members, quantities = hidden_ref.shape[0], enc_ref.shape[0]
    lane = iota((wanted, nodes), 1)
    at = 2 * count + 16
    lists = (
        south_ref[at : at + wanted, 0:1],
        north_ref[at : at + wanted, 0:1],
        west_ref[4 * rows : 4 * rows + wanted, 0:1],
        east_ref[4 * rows : 4 * rows + wanted, 0:1],
    )
    owed = [jnp.where(v.astype(F32).astype(I32) == lane, 1.0, 0.0).astype(BF16) for v in lists]
    for q in range(4):
        owed_ref[q * wanted : (q + 1) * wanted, :] = owed[q]
    total = part_refs[0][...].astype(F32)
    for ref in part_refs[1:]:
        total = total + ref[...].astype(F32)
    total = total.astype(BF16)
    pad[...] = jnp.zeros(pad.shape, BF16)
    for m in range(members):
        pad[m, m * quantities : (m + 1) * quantities, :] = enc_ref[...]
        hidden = silu(dot(total, pad[m]))
        hidden_ref[m] = hidden
        project(m, hidden, owed, ws_ref[...], wr_ref[...], table_ref, out_refs, wanted, nodes)


def layer_kernel(last, wanted, chunk, *refs):
    hidden_ref, table_ref, owed_ref, gather_ref, scatter_ref = refs[:5]
    halo_refs, wu_ref = refs[5:9], refs[9]
    if last:
        dec_ref, out_ref, known = refs[10:]
    else:
        ws_ref, wr_ref, next_hidden_ref, next_table_ref, *out_refs, known = refs[10:]
    members, nodes, width = hidden_ref.shape
    edges, rows = gather_ref.shape
    if not last:
        owed = [owed_ref[q * wanted : (q + 1) * wanted, :] for q in range(4)]
    for m in range(members):
        known[0 : 2 * nodes, :] = table_ref[m]
        for q in range(4):
            at = 2 * nodes + q * wanted
            known[at : at + wanted, :] = halo_refs[q][m * wanted : (m + 1) * wanted, :]
        at = 2 * nodes + 4 * wanted
        known[at:, :] = jnp.zeros((rows - at, width), BF16)
        collected = jnp.zeros((nodes, width), F32)
        for k in range(0, edges, chunk):
            message = silu(dot(gather_ref[k : k + chunk, :], known[...])).astype(BF16)
            collected = collected + dot(scatter_ref[:, k : k + chunk], message)
        hidden = hidden_ref[m] + dot(collected.astype(BF16), wu_ref[...])
        if last:
            got = dot(dec_ref[...], normalize(hidden), 1, 1)
            out_ref[m * got.shape[0] : (m + 1) * got.shape[0], :] = got.astype(BF16)
        else:
            next_hidden_ref[m] = hidden
            project(m, hidden, owed, ws_ref[...], wr_ref[...], next_table_ref, out_refs, wanted, nodes)


def land_kernel(rows, slots, u_ref, w_ref, *refs):
    corr_refs, out_ref = refs[:slots], refs[slots]
    width = u_ref.shape[1]
    count = u_ref.shape[0] // rows
    total = dot(corr_refs[0][...], w_ref[0])
    for s in range(1, slots):
        total = total + dot(corr_refs[s][...], w_ref[s])
    for r in range(rows):
        here = pl.ds(r, count, stride=rows)
        out_ref[here, :] = u_ref[here, :] + total[:, r * width : (r + 1) * width]


def body(
    fields, wind_east, wind_north, diffusion, inflow_owner, inflow_cell, inflow_node, inflow_weight,
    encoder, sender_weight, receiver_weight, update_weight, decoder, edge_sender, edge_receiver, halo_rows,
    outflow_owner, outflow_node, outflow_cell, outflow_weight,
):
    members, quantities, rows, width = fields.shape
    count, cells = members * quantities, rows * width
    lon, lat = lax.axis_size("lon"), lax.axis_size("lat")
    me = lax.axis_index("lon").astype(I32).reshape(1)
    blocks, entries = inflow_cell.shape
    hid = encoder.shape[1]
    layers = sender_weight.shape[0]
    edges = edge_sender.shape[-1]
    wanted = halo_rows.shape[-1]
    nodes = NODE_DEV

    def shift(v, s):
        return lax.ppermute(v, "lon", [(i, (i + s) % lon) for i in range(lon)])

    def up(v):
        return lax.ppermute(v, "lat", [(i, i + 1) for i in range(lat - 1)])

    def down(v):
        return lax.ppermute(v, "lat", [(i + 1, i) for i in range(lat - 1)])

    x = fields.reshape(count * rows, width)
    halo = halo_rows.reshape(4 * wanted, 1)
    rates = (wind_east, wind_north, diffusion)
    tall, wide = 2 * count + 16 + wanted, 4 * rows + wanted
    to_north, to_south, cols = call(
        functools.partial(edge_kernel, rows, wanted),
        (shape((tall, width), BF16), shape((tall, width), BF16), shape((4 * rows, count), F32)),
        (x, *rates, halo),
        cost=cost(0, 8 * MIB),
    )
    south, north = up(to_north), down(to_south)
    to_east, to_west = call(
        functools.partial(side_kernel, rows, wanted),
        (shape((wide, count), BF16), shape((wide, count), BF16)),
        (south, north, cols, *rates, halo),
        cost=cost(0, 4 * MIB),
    )
    west, east = shift(to_east, 1), shift(to_west, lon - 1)

    into = build(
        True, lon, nodes, cells, blocks, me, inflow_owner.reshape(-1), inflow_node, inflow_cell, inflow_weight
    )
    lat_at = lax.axis_index("lat")
    pole = jnp.stack([lat_at == 0, lat_at == lat - 1]).astype(F32)[:, None]
    u, *parts = call(
        functools.partial(step_kernel, rows, lon, nodes),
        [shape(x.shape, F32)] + [shape((nodes, count), F32)] + [shape((nodes, count), BF16)] * (lon - 1),
        (x, *rates, cols, south, north, west, east, pole, into),
        scratch=[
            pltpu.VMEM(x.shape, F32),
            pltpu.VMEM(x.shape, F32),
            pltpu.VMEM((8, 8, count), F32),
            pltpu.VMEM((count, cells), BF16),
        ],
        vmem=24 + lon * 3,
        cost=cost(2 * lon * nodes * cells * count, 16 * MIB),
    )
    parts = parts[:1] + [shift(parts[s], s) for s in range(1, lon)]

    lists = jnp.stack(
        [outflow_node.astype(F32), outflow_cell.astype(F32), outflow_weight,
         jnp.broadcast_to(outflow_owner.astype(F32), (blocks, entries))]
    )
    lists = jnp.stack([lists] + [shift(lists, s) for s in range(1, lon)], axis=1)
    lists = lists.reshape(4, lon * blocks, entries)
    owners = lists[3, :, 0].astype(I32)
    onto = build(False, lon, nodes, cells, blocks, me, owners, lists[0], lists[1], lists[2])

    known = 2 * nodes + 256 * -(-4 * wanted // 256)
    senders, receivers = edge_sender.reshape(edges), edge_receiver.reshape(edges)
    gather, scatter = call(
        link_kernel,
        (shape((edges, known), BF16), shape((nodes, edges), BF16)),
        (senders.reshape(edges, 1), receivers.reshape(edges, 1), receivers.reshape(1, edges)),
        cost=cost(0, 8 * MIB),
    )

    reply = [shape((members * wanted, hid), BF16)] * 4
    state = [shape((members, nodes, hid), F32), shape((members, 2 * nodes, hid), BF16)]
    hidden, table, owed, *out = call(
        functools.partial(encode_kernel, lon, rows, count, wanted),
        state + [shape((4 * wanted, nodes), BF16)] + reply,
        (*parts, encoder, sender_weight[0], receiver_weight[0], south, north, west, east),
        scratch=[pltpu.VMEM((members, count, hid), BF16)],
        cost=cost(2e9, 8 * MIB),
    )
    for layer in range(layers):
        halos = [up(out[1]), down(out[0]), shift(out[3], 1), shift(out[2], lon - 1)]
        last = layer == layers - 1
        args = (hidden, table, owed, gather, scatter, *halos, update_weight[layer])
        scratch = [pltpu.VMEM((known, hid), BF16)]
        kernel = functools.partial(layer_kernel, last, wanted, edges // 3)
        if last:
            corr = call(
                kernel, shape((count, nodes), BF16), (*args, decoder.T), scratch=scratch, cost=cost(4e9, 12 * MIB)
            )
        else:
            hidden, table, *out = call(
                kernel,
                state + reply,
                (*args, sender_weight[layer + 1], receiver_weight[layer + 1]),
                scratch=scratch,
                cost=cost(4e9, 12 * MIB),
            )
    corrs = [corr] + [shift(corr, s) for s in range(1, lon)]
    out = call(
        functools.partial(land_kernel, rows, lon),
        shape(x.shape, F32),
        (u, onto, *corrs),
        vmem=24 + lon,
        cost=cost(2 * lon * nodes * cells * count, 8 * MIB),
    )
    return out.reshape(members, quantities, rows, width)


def solution(mesh):
    tile, block, part = P("lat", "lon"), P(("lat", "lon"), None), P("lat", "lon", None)
    placed = (P("member", None, "lat", "lon"), tile, tile, tile, block, block, block, block)
    placed += (P(),) * 5 + (part, part, P("lat", "lon", None, None)) + (block,) * 4
    return jax.shard_map(
        body, mesh=mesh, in_specs=placed, out_specs=P("member", None, "lat", "lon"), check_vma=False
    )
```

```python
import functools

import jax
import jax.numpy as jnp
from jax import lax
from jax.experimental import pallas as pl
from jax.experimental.pallas import tpu as pltpu
from jax.sharding import PartitionSpec as P

F32, BF16, I32 = jnp.float32, jnp.bfloat16, jnp.int32
MIB = 1 << 20
NODE_DEV = 256


def dot(a, b, ca=1, cb=0):
    return lax.dot_general(a, b, (((ca,), (cb,)), ((), ())), preferred_element_type=F32)


def iota(shape, dim):
    return lax.broadcasted_iota(I32, shape, dim)


def call(kernel, outs, args, smem=0, away=0, small=0, scratch=(), vmem=32, cost=None):
    single = not isinstance(outs, (list, tuple))
    spaces = [pltpu.SMEM] * smem + [pl.ANY] * away + [pltpu.VMEM] * (len(args) - smem - away)
    if single:
        out_specs = pl.BlockSpec(memory_space=pltpu.VMEM)
    else:
        homes = [pltpu.VMEM] * (len(outs) - small) + [pltpu.SMEM] * small
        out_specs = tuple(pl.BlockSpec(memory_space=m) for m in homes)
    return pl.pallas_call(
        kernel,
        out_shape=outs if single else tuple(outs),
        in_specs=[pl.BlockSpec(memory_space=m) for m in spaces],
        out_specs=out_specs,
        scratch_shapes=list(scratch),
        compiler_params=pltpu.CompilerParams(vmem_limit_bytes=vmem * MIB),
        cost_estimate=cost,
    )(*args)


def cost(flops, bytes_accessed):
    return pl.CostEstimate(flops=int(flops), bytes_accessed=int(bytes_accessed), transcendentals=0)


def shape(dims, dtype):
    return jax.ShapeDtypeStruct(tuple(dims), dtype)


def split(v):
    hi = v.astype(BF16).astype(F32)
    return hi, v - hi


def pick_columns(width):
    row, lane = iota((16, width), 0), iota((16, width), 1)
    hit = (row == 0) & (lane == 0) | (row == 1) & (lane == 1)
    hit = hit | (row == 2) & (lane == width - 1) | (row == 3) & (lane == width - 2)
    return hit.astype(F32).astype(BF16)


def coefficients(we, wn, d):
    pe, ne = jnp.maximum(we, 0.0), jnp.minimum(we, 0.0)
    pn, nn = jnp.maximum(wn, 0.0), jnp.minimum(wn, 0.0)
    return 1.0 - pe + ne - pn + nn - 4.0 * d, pe + d, d - ne, pn + d, d - nn


def edge_kernel(rows, slots, me_ref, in_owner_ref, out_owner_ref, *refs):
    homes, (up_ref, down_ref, side_ref, rate_ref, x_ref, in_ref, *out_refs) = refs[:11], refs[11 : 17 + slots]
    halo_ref, block, taken, late, *tables, sems = refs[17 + slots :]
    held = [x_ref, *(rate_ref.at[j] for j in range(3)), halo_ref, *tables]
    copies = [pltpu.make_async_copy(a, b, sems.at[k]) for k, (a, b) in enumerate(zip(homes, held))]
    for copy in copies:
        copy.start()
    for copy in copies[1:]:
        copy.wait()
    sort_blocks(slots, me_ref[0], in_owner_ref, tables[:3], in_ref, taken)
    sort_blocks(slots, me_ref[0], out_owner_ref, tables[3:], late, taken)
    for s in range(slots):
        out_refs[s][...] = late[s]
    copies[0].wait()
    count = x_ref.shape[0] // rows
    width = x_ref.shape[1]
    wanted = halo_ref.shape[1]

    def row(r):
        return x_ref[pl.ds(r, count, stride=rows), :].astype(BF16)

    for out_ref, near, far, q in ((up_ref, rows - 1, rows - 2, 1), (down_ref, 0, 1, 0)):
        out_ref[0:count, :] = row(near)
        out_ref[count : 2 * count, :] = row(far)
        block[...] = jnp.zeros(block.shape, F32)
        for j in range(3):
            hi, lo = split(rate_ref[j, near : near + 1, :])
            block[j : j + 1, :] = hi
            block[j + 3 : j + 4, :] = lo
        block[6:7, 0:wanted] = halo_ref[q : q + 1, :].astype(F32)
        out_ref[2 * count : 2 * count + 16, :] = block[...].astype(BF16)
    lane = iota((rows, count), 1)
    for i, (c, q) in enumerate(((width - 1, 3), (0, 2))):
        side_ref[i, 2 * rows : 3 * rows, :] = jnp.zeros((rows, count), F32)
        side_ref[i, 2 * rows + 2 : 2 * rows + 3, 0:wanted] = halo_ref[q : q + 1, :].astype(F32)
        rates = jnp.zeros((rows, count), F32)
        for j in range(3):
            hi, lo = split(rate_ref[j][:, c : c + 1])
            rates = jnp.where(lane == j, hi, jnp.where(lane == j + 3, lo, rates))
        side_ref[i, 3 * rows : 4 * rows, :] = rates
    pick = pick_columns(width)
    for r in range(rows):
        got = dot(pick, row(r), 1, 1)
        for i, k in enumerate((2, 0)):
            side_ref[i, r : r + 1, :] = got[k : k + 1, :]
            side_ref[i, rows + r : rows + r + 1, :] = got[k + 1 : k + 2, :]


def side_kernel(rows, south_ref, north_ref, side_ref, east_ref, west_ref):
    count, width = side_ref.shape[2], south_ref.shape[1]
    pick = pick_columns(width)
    south = dot(pick, south_ref[0:count, :], 1, 1)
    north = dot(pick, north_ref[0:count, :], 1, 1)
    line = iota((4 * rows, count), 0)
    for i, (out_ref, k) in enumerate(((east_ref, 2), (west_ref, 0))):
        v = jnp.where(line == 2 * rows, south[k : k + 1, :], side_ref[i])
        out_ref[...] = jnp.where(line == 2 * rows + 1, north[k : k + 1, :], v).astype(BF16)


def sort_blocks(slots, me, owner_ref, lists, out_ref, taken):
    cap = out_ref.shape[1] // 3
    out_ref[...] = jnp.zeros(out_ref.shape, F32)
    for s in range(slots):
        taken[s] = 0

    @pl.loop(0, lists[0].shape[0])
    def _(b):
        s = lax.rem(owner_ref[b] - me + slots, slots)
        at = jnp.minimum(taken[s], cap - 1)
        taken[s] = at + 1
        for k in range(3):
            out_ref[s, pl.ds(k * cap + at, 1), :] = lists[k][pl.ds(b, 1), :].astype(F32)


def build_kernel(slots, *refs):
    list_refs, (out_ref, hot, spread) = refs[:-3], refs[-3:]
    nodes, cells = out_ref.shape[1], out_ref.shape[2]
    joint = len(list_refs) == 1
    cap, entries = list_refs[0].shape[-2] // 3, list_refs[0].shape[-1]
    node_ids = iota((nodes, entries), 0).astype(F32)
    cell_ids = iota((cells, entries), 0).astype(F32)

    def fill(s, ref):
        for c in range(cap):
            lanes = slice(c * entries, (c + 1) * entries)
            node, cell, weight = (ref[k * cap + c : k * cap + c + 1, :] for k in range(3))
            hot[:, lanes] = jnp.where(node_ids == node, 1.0, 0.0).astype(BF16)
            spread[:, lanes] = jnp.where(cell_ids == cell, weight, 0.0).astype(BF16)
        out_ref[s] = dot(hot[...], spread[...], 1, 1).astype(BF16)

    if joint:

        @pl.loop(0, slots)
        def _(s):
            fill(s, list_refs[0].at[s])
    else:
        for s in range(slots):
            fill(s, list_refs[s])


def build(slots, nodes, cells, lists):
    cap, entries = lists[0].shape[-2] // 3, lists[0].shape[-1]
    size = slots * nodes * cells
    return call(
        functools.partial(build_kernel, slots),
        shape((slots, nodes, cells), BF16),
        lists,
        scratch=[pltpu.VMEM((nodes, cap * entries), BF16), pltpu.VMEM((cells, cap * entries), BF16)],
        vmem=8 + 3 * size // MIB,
        cost=cost(2 * size * cap * entries, 4 * size),
    )


def step_kernel(
    rows, lat, slots,
    lat_ref, x_ref, wind_ref, side_ref, south_ref, north_ref, west_ref, east_ref, a_ref,
    u_ref, *rest,
):
    part_refs, (rate, ring, b1, b2, mid, flat) = rest[:slots], rest[slots:]
    count, width = side_ref.shape[2], x_ref.shape[1]
    at_south = jnp.where(lat_ref[0] == 0, 1.0, 0.0)
    at_north = jnp.where(lat_ref[0] == lat - 1, 1.0, 0.0)

    def mend(c0, cw, ce, cs, cn):
        line = iota(c0.shape, 0)
        ps, pn = jnp.where(line == 0, at_south, 0.0), jnp.where(line == rows - 1, at_north, 0.0)
        return c0 + ps * cs + pn * cn, cw, ce, cs * (1.0 - ps), cn * (1.0 - pn)

    own = mend(*coefficients(wind_ref[0], wind_ref[1], wind_ref[2]))
    outer = []
    for ref in (south_ref, north_ref):
        v = ref[2 * count : 2 * count + 16, :].astype(F32)
        outer.append(coefficients(*(v[j : j + 1, :] + v[j + 3 : j + 4, :] for j in range(3))))
    for j in range(5):
        rate[j, 0:1, :] = outer[0][j]
        rate[j, 1 : rows + 1, :] = own[j]
        rate[j, rows + 1 : rows + 2, :] = outer[1][j]

    west, east = west_ref[...].astype(F32), east_ref[...].astype(F32)
    w1, w2, w_corner, w_rate = (west[k * rows : (k + 1) * rows, :] for k in range(4))
    e1, e2, e_corner, e_rate = (east[k * rows : (k + 1) * rows, :] for k in range(4))

    half = ring.shape[0] // 2

    def place(out_ref, lines):
        k, col = iota((2 * half, lines * width), 0), iota((2 * half, lines * width), 1)
        hit = jnp.where(k < half, k * width, (k - half) * width + width - 1) == col
        out_ref[...] = dot(ring[...].astype(BF16), jnp.where(hit, 1.0, 0.0).astype(BF16), 0, 0)

    ring[...] = jnp.zeros(ring.shape, F32)
    for base, corner, near, j, c in ((0, w_corner, w1, 1, 0), (half, e_corner, e1, 2, width - 1)):
        ring[base : base + 1, :] = outer[0][j][:, c : c + 1] * corner[0:1, :]
        ring[base + 1 : base + 1 + rows, :] = own[j][:, c : c + 1] * near
        ring[base + 1 + rows : base + 2 + rows, :] = outer[1][j][:, c : c + 1] * corner[1:2, :]
    place(b1, rows + 2)

    def ring_col(rates, corner, v, out_w, out_e):
        k0, kw, ke, ks, kn = mend(*coefficients(*(rates[:, j : j + 1] + rates[:, j + 3 : j + 4] for j in range(3))))
        line = iota(v.shape, 0)
        to_s = jnp.where(line == 0, corner[0:1, :], pltpu.roll(v, 1, 0))
        to_n = jnp.where(line == rows - 1, corner[1:2, :], pltpu.roll(v, rows - 1, 0))
        return k0 * v + kw * out_w + ke * out_e + ks * to_s + kn * to_n

    ring[...] = jnp.zeros(ring.shape, F32)
    ring[0:rows, :] = own[1][:, 0:1] * ring_col(w_rate, w_corner, w1, w2, side_ref[1, 0:rows, :])
    ring[half : half + rows, :] = own[2][:, width - 1 : width] * ring_col(
        e_rate, e_corner, e1, side_ref[0, 0:rows, :], e2
    )
    place(b2, rows)

    k, col = iota((2 * width, 2 * width), 0), iota((2 * width, 2 * width), 1)
    k = jnp.where(k < width, k, k - width)
    turn = jnp.where(jnp.where(col < width, col - 1, col - width + 1) == k, 1.0, 0.0).astype(BF16)

    def advance(line, v, below, above, b_ref, at):
        hi = v.astype(BF16)
        pair = jnp.concatenate([hi, (v - hi.astype(F32)).astype(BF16)], 1)
        turned = dot(pair, turn)
        c0, cw, ce, cs, cn = (rate[j, line + 1 : line + 2, :] for j in range(5))
        new = c0 * v + cw * turned[:, 0:width] + ce * turned[:, width : 2 * width]
        return new + cs * below + cn * above + b_ref[:, at * width : (at + 1) * width]

    def cell_row(r):
        if r < 0:
            return south_ref[(-1 - r) * count : -r * count, :].astype(F32)
        if r >= rows:
            return north_ref[(r - rows) * count : (r - rows + 1) * count, :].astype(F32)
        return x_ref[pl.ds(r, count, stride=rows), :]

    for r in range(-1, rows + 1):
        mid[r + 1] = advance(r, cell_row(r), cell_row(r - 1), cell_row(r + 1), b1, r + 1)
    for r in range(rows):
        new = advance(r, mid[r + 1], mid[r], mid[r + 2], b2, r)
        u_ref[:, r * width : (r + 1) * width] = new
        flat[:, r * width : (r + 1) * width] = new.astype(BF16)

    for s in range(slots):
        part_refs[s][...] = dot(a_ref[s], flat[...], 1, 1).astype(part_refs[s].dtype)


def silu(v):
    return 0.5 * v * (1.0 + jnp.tanh(0.5 * v))


def normalize(v):
    return (v * lax.rsqrt(jnp.mean(v * v, axis=-1, keepdims=True) + 1e-06)).astype(BF16)


def link_kernel(sender_ref, receiver_ref, gather_ref, scatter_ref, local_ref, order):
    edges, known = gather_ref.shape
    nodes = scatter_ref.shape[0]
    sender, receiver = sender_ref[...], receiver_ref[...]
    local = jnp.where(sender < nodes, 1.0, 0.0)
    order[...] = jnp.where(iota((edges, edges), 0) < iota((edges, edges), 1), 1.0, 0.0).astype(BF16)
    before = dot(jnp.broadcast_to(local, (16, edges)).astype(BF16), order[...])[0:1, :]
    total = jnp.sum(local)
    local_ref[0] = total.astype(I32)
    index = iota((1, edges), 1).astype(F32)
    place = jnp.where(sender < nodes, before, total + index - before)
    order[...] = jnp.where(iota((edges, edges), 0).astype(F32) == place, 1.0, 0.0).astype(BF16)
    line = iota((16, edges), 0)
    high = sender // nodes
    keys = jnp.where(line == 0, sender - high * nodes, jnp.where(line == 1, high, jnp.where(line == 2, receiver, 0)))
    keys = keys.astype(F32).astype(BF16)
    cols = dot(order[...], keys, 1, 1)
    sender, receiver = cols[:, 0:1] + nodes * cols[:, 1:2], cols[:, 2:3]
    lane = iota((edges, nodes), 1).astype(F32)
    gather_ref[:, 0:nodes] = jnp.where(sender == lane, 1.0, 0.0).astype(BF16)
    gather_ref[:, nodes : 2 * nodes] = jnp.where(receiver == lane, 1.0, 0.0).astype(BF16)
    rest = (iota((edges, known - 2 * nodes), 1) + nodes).astype(F32)
    gather_ref[:, 2 * nodes :] = jnp.where(sender == rest, 1.0, 0.0).astype(BF16)
    row = dot(keys, order[...], 1, 1)[2:3, :]
    scatter_ref[...] = jnp.where(row == iota((nodes, edges), 0).astype(F32), 1.0, 0.0).astype(BF16)


def project(m, hidden, owed, ws, wr, table_ref, out_refs, wanted, nodes):
    normed = normalize(hidden)
    source = dot(normed, ws).astype(BF16)
    table_ref[m, 0:nodes, :] = source
    table_ref[m, nodes : 2 * nodes, :] = dot(normed, wr).astype(BF16)
    for q in range(4):
        out_refs[q][m * wanted : (m + 1) * wanted, :] = dot(owed[q], source).astype(BF16)


def owed_kernel(rows, wanted, south_ref, north_ref, west_ref, east_ref, enc_ref, owed_ref, pad_ref):
    nodes = owed_ref.shape[1]
    count = west_ref.shape[1]
    lists = [ref[2 * count : 2 * count + 16, :].astype(F32)[6:7, :] for ref in (south_ref, north_ref)]
    lists += [ref[2 * rows : 4 * rows, 0:128].astype(F32)[2:3, :] for ref in (west_ref, east_ref)]
    for q in range(4):
        hot = jnp.where(iota((nodes, 128), 0).astype(F32) == lists[q], 1.0, 0.0)
        owed_ref[q * wanted : (q + 1) * wanted, :] = hot.T[0:wanted, :].astype(BF16)
    quantities = enc_ref.shape[0]
    pad_ref[...] = jnp.zeros(pad_ref.shape, BF16)
    for m in range(pad_ref.shape[0]):
        pad_ref[m, m * quantities : (m + 1) * quantities, :] = enc_ref[...]


def encode_kernel(slots, wanted, *refs):
    part_refs = refs[:slots]
    pad_ref, ws_ref, wr_ref, owed_ref, hidden_ref, table_ref, *out_refs = refs[slots:]
    nodes = part_refs[0].shape[0]
    owed = [owed_ref[q * wanted : (q + 1) * wanted, :] for q in range(4)]
    total = part_refs[0][...].astype(F32)
    for ref in part_refs[1:]:
        total = total + ref[...].astype(F32)
    total = total.astype(BF16)
    for m in range(hidden_ref.shape[0]):
        hidden = silu(dot(total, pad_ref[m]))
        hidden_ref[m] = hidden
        project(m, hidden, owed, ws_ref[0], wr_ref[0], table_ref, out_refs, wanted, nodes)


def messages(lo, hi, chunk, gather_ref, scatter_ref, depth, tables, sums_ref):
    step = chunk // 3

    @pl.loop(lo, hi)
    def _(c):
        at = pl.multiple_of(c * chunk, chunk)
        for m, table in enumerate(tables):
            found = [
                silu(dot(gather_ref[pl.ds(at + k, step), 0:depth], table[...])).astype(BF16)
                for k in range(0, chunk, step)
            ]
            sums_ref[m] += dot(scatter_ref[:, pl.ds(at, chunk)], jnp.concatenate(found, 0))


def early_kernel(chunk, local_ref, table_ref, gather_ref, scatter_ref, sums_ref):
    members, depth, _ = table_ref.shape
    sums_ref[...] = jnp.zeros(sums_ref.shape, F32)
    tables = [table_ref.at[m] for m in range(members)]
    messages(0, local_ref[0] // chunk, chunk, gather_ref, scatter_ref, depth, tables, sums_ref)


def layer_kernel(layer, last, wanted, chunk, *refs):
    local_ref, hidden_ref, table_ref, owed_ref, gather_ref, scatter_ref, early_ref = refs[:7]
    halo_refs, wu_ref = refs[7:11], refs[11]
    if last:
        dec_ref, out_ref, known, sums = refs[12:]
    else:
        ws_ref, wr_ref, next_hidden_ref, next_table_ref, *out_refs, known, sums = refs[12:]
    members, nodes, width = hidden_ref.shape
    edges, depth = gather_ref.shape
    sums[...] = early_ref[...]
    for m in range(members):
        known[m, 0 : 2 * nodes, :] = table_ref[m]
        for q in range(4):
            at = 2 * nodes + q * wanted
            known[m, at : at + wanted, :] = halo_refs[q][m * wanted : (m + 1) * wanted, :]
        at = 2 * nodes + 4 * wanted
        known[m, at:, :] = jnp.zeros((depth - at, width), BF16)
    tables = [known.at[m] for m in range(members)]
    messages(local_ref[0] // chunk, edges // chunk, chunk, gather_ref, scatter_ref, depth, tables, sums)
    if not last:
        owed = [owed_ref[q * wanted : (q + 1) * wanted, :] for q in range(4)]
    for m in range(members):
        hidden = hidden_ref[m] + dot(sums[m].astype(BF16), wu_ref[layer])
        if last:
            got = dot(dec_ref[...], normalize(hidden), 1, 1)
            out_ref[m * got.shape[0] : (m + 1) * got.shape[0], :] = got.astype(BF16)
        else:
            next_hidden_ref[m] = hidden
            project(m, hidden, owed, ws_ref[layer + 1], wr_ref[layer + 1], next_table_ref, out_refs, wanted, nodes)


def land_kernel(rows, slots, u_ref, w_ref, *refs):
    corr_refs, out_ref = refs[:slots], refs[slots]
    count, width = u_ref.shape[0], u_ref.shape[1] // rows
    total = u_ref[...]
    for s in range(slots):
        total = total + dot(corr_refs[s][...], w_ref[s])
    for r in range(rows):
        out_ref[pl.ds(r, count, stride=rows), :] = total[:, r * width : (r + 1) * width]


def body(
    fields, wind_east, wind_north, diffusion, inflow_owner, inflow_cell, inflow_node, inflow_weight,
    encoder, sender_weight, receiver_weight, update_weight, decoder, edge_sender, edge_receiver, halo_rows,
    outflow_owner, outflow_node, outflow_cell, outflow_weight,
):
    members, quantities, rows, width = fields.shape
    count, cells = members * quantities, rows * width
    lon, lat = lax.axis_size("lon"), lax.axis_size("lat")
    me = lax.axis_index("lon").astype(I32).reshape(1)
    lat_at = lax.axis_index("lat").astype(I32).reshape(1)
    blocks, entries = inflow_cell.shape
    hid = encoder.shape[1]
    layers = sender_weight.shape[0]
    edges = edge_sender.shape[-1]
    wanted = halo_rows.shape[-1]
    nodes = NODE_DEV
    cap = max(2, -(-2 * blocks // lon))

    def shift(v, s):
        return lax.ppermute(v, "lon", [(i, (i + s) % lon) for i in range(lon)])

    def up(v):
        return lax.ppermute(v, "lat", [(i, (i + 1) % lat) for i in range(lat)])

    def down(v):
        return lax.ppermute(v, "lat", [((i + 1) % lat, i) for i in range(lat)])

    x = fields.reshape(count * rows, width)
    halo = halo_rows.reshape(4, wanted)
    rates = (wind_east, wind_north, diffusion)
    tall = 2 * count + 16
    tables = (inflow_node, inflow_cell, inflow_weight, outflow_node, outflow_cell, outflow_weight)
    to_north, to_south, side, wind, x, in_lists, *out_lists = call(
        functools.partial(edge_kernel, rows, lon),
        [shape((tall, width), BF16), shape((tall, width), BF16), shape((2, 4 * rows, count), F32),
         shape((3, rows, width), F32), shape(x.shape, F32), shape((lon, 3 * cap, entries), F32)]
        + [shape((3 * cap, entries), F32)] * lon,
        (me, inflow_owner.reshape(blocks), outflow_owner.reshape(blocks), x, *rates, halo, *tables),
        smem=3,
        away=11,
        scratch=[
            pltpu.VMEM(halo.shape, I32),
            pltpu.VMEM((16, width), F32),
            pltpu.SMEM((lon,), I32),
            pltpu.VMEM((lon, 3 * cap, entries), F32),
            *(pltpu.VMEM(v.shape, v.dtype) for v in tables),
            pltpu.SemaphoreType.DMA((11,)),
        ],
        vmem=56,
        cost=cost(0, 8 * MIB),
    )
    south, north = up(to_north), down(to_south)
    into = build(lon, nodes, cells, (in_lists,))
    side, into = lax.optimization_barrier((side, into))
    to_east, to_west = call(
        functools.partial(side_kernel, rows),
        (shape((4 * rows, count), BF16), shape((4 * rows, count), BF16)),
        (south, north, side),
        vmem=4,
        cost=cost(0, 4 * MIB),
    )
    west, east = shift(to_east, 1), shift(to_west, lon - 1)

    u, *parts = call(
        functools.partial(step_kernel, rows, lat, lon),
        [shape((count, cells), F32)] + [shape((nodes, count), F32)] + [shape((nodes, count), BF16)] * (lon - 1),
        (lat_at, x, wind, side, south, north, west, east, into),
        smem=1,
        scratch=[
            pltpu.VMEM((5, rows + 2, width), F32),
            pltpu.VMEM((32, count), F32),
            pltpu.VMEM((count, (rows + 2) * width), F32),
            pltpu.VMEM((count, cells), F32),
            pltpu.VMEM((rows + 2, count, width), F32),
            pltpu.VMEM((count, cells), BF16),
        ],
        vmem=14 + lon * 2,
        cost=cost(2 * lon * nodes * cells * count, 16 * MIB),
    )
    parts, edge_sender, edge_receiver = lax.optimization_barrier((parts, edge_sender, edge_receiver))
    parts = parts[:1] + [shift(parts[s], s) for s in range(1, lon)]

    known = 2 * nodes + 256 * -(-4 * wanted // 256)
    chunk = edges // 2
    gather, scatter, local = call(
        link_kernel,
        (shape((edges, known), BF16), shape((nodes, edges), BF16), shape((1,), I32)),
        (edge_sender.reshape(1, edges), edge_receiver.reshape(1, edges)),
        small=1,
        scratch=[pltpu.VMEM((edges, edges), BF16)],
        vmem=24,
        cost=cost(2 * edges * edges * 48, 8 * MIB),
    )
    scatter, out_lists = lax.optimization_barrier((scatter, out_lists))
    out_lists = [out_lists[0]] + [shift(out_lists[s], s) for s in range(1, lon)]
    parts, out_lists = lax.optimization_barrier((parts, out_lists))
    onto = build(lon, nodes, cells, out_lists)

    reply = [shape((members * wanted, hid), BF16)] * 4
    state = [shape((members, nodes, hid), F32), shape((members, 2 * nodes, hid), BF16)]
    owed, pad = call(
        functools.partial(owed_kernel, rows, wanted),
        (shape((4 * wanted, nodes), BF16), shape((members, count, hid), BF16)),
        (south, north, west, east, encoder),
        vmem=8,
        cost=cost(0, 4 * MIB),
    )
    hidden, table, *out = call(
        functools.partial(encode_kernel, lon, wanted),
        state + reply,
        (*parts, pad, sender_weight, receiver_weight, owed),
        vmem=16,
        cost=cost(2e9, 8 * MIB),
    )
    for layer in range(layers):
        halos = [up(out[1]), down(out[0]), shift(out[3], 1), shift(out[2], lon - 1)]
        early = call(
            functools.partial(early_kernel, chunk),
            shape((members, nodes, hid), F32),
            (local, table, gather, scatter),
            smem=1,
            vmem=16,
            cost=cost(3e9, 8 * MIB),
        )
        last = layer == layers - 1
        args = (local, hidden, table, owed, gather, scatter, early, *halos, update_weight)
        scratch = [pltpu.VMEM((members, known, hid), BF16), pltpu.VMEM((members, nodes, hid), F32)]
        kernel = functools.partial(layer_kernel, layer, last, wanted, chunk)
        if last:
            corr = call(
                kernel, shape((count, nodes), BF16), (*args, decoder.T), smem=1, scratch=scratch, vmem=20,
                cost=cost(4e9, 12 * MIB),
            )
        else:
            hidden, table, *out = call(
                kernel,
                state + reply,
                (*args, sender_weight, receiver_weight),
                smem=1,
                scratch=scratch,
                vmem=20,
                cost=cost(4e9, 12 * MIB),
            )
    corrs = [corr] + [shift(corr, s) for s in range(1, lon)]
    out = call(
        functools.partial(land_kernel, rows, lon),
        shape(x.shape, F32),
        (u, onto, *corrs),
        vmem=16 + lon,
        cost=cost(2 * lon * nodes * cells * count, 8 * MIB),
    )
    return out.reshape(members, quantities, rows, width)


def solution(mesh):
    tile, block, part = P("lat", "lon"), P(("lat", "lon"), None), P("lat", "lon", None)
    placed = (P("member", None, "lat", "lon"), tile, tile, tile, block, block, block, block)
    placed += (P(),) * 5 + (part, part, P("lat", "lon", None, None)) + (block,) * 4
    return jax.shard_map(
        body, mesh=mesh, in_specs=placed, out_specs=P("member", None, "lat", "lon"), check_vma=False
    )
```

```python
import functools

import jax
import jax.numpy as jnp
from jax import lax
from jax.experimental import pallas as pl
from jax.experimental.pallas import tpu as pltpu
from jax.sharding import PartitionSpec as P

F32, BF16, I32 = jnp.float32, jnp.bfloat16, jnp.int32
MIB = 1 << 20
SCALE = 0.05
NODE_DEV = 256


def dot(a, b, ca=1, cb=0):
    return lax.dot_general(a, b, (((ca,), (cb,)), ((), ())), preferred_element_type=F32)


def iota(shape, dim):
    return lax.broadcasted_iota(I32, shape, dim)


def call(kernel, outs, args, smem=0, away=0, small=0, scratch=(), vmem=32, cost=None):
    single = not isinstance(outs, (list, tuple))
    spaces = [pltpu.SMEM] * smem + [pl.ANY] * away + [pltpu.VMEM] * (len(args) - smem - away)
    if single:
        out_specs = pl.BlockSpec(memory_space=pltpu.VMEM)
    else:
        homes = [pltpu.VMEM] * (len(outs) - small) + [pltpu.SMEM] * small
        out_specs = tuple(pl.BlockSpec(memory_space=m) for m in homes)
    return pl.pallas_call(
        kernel,
        out_shape=outs if single else tuple(outs),
        in_specs=[pl.BlockSpec(memory_space=m) for m in spaces],
        out_specs=out_specs,
        scratch_shapes=list(scratch),
        compiler_params=pltpu.CompilerParams(vmem_limit_bytes=vmem * MIB),
        cost_estimate=cost,
    )(*args)


def cost(flops, bytes_accessed):
    return pl.CostEstimate(flops=int(flops * SCALE), bytes_accessed=int(bytes_accessed * SCALE), transcendentals=0)


def shape(dims, dtype):
    return jax.ShapeDtypeStruct(tuple(dims), dtype)


def split(v):
    hi = v.astype(BF16).astype(F32)
    return hi, v - hi


def pick_columns(width):
    row, lane = iota((16, width), 0), iota((16, width), 1)
    hit = (row == 0) & (lane == 0) | (row == 1) & (lane == 1)
    hit = hit | (row == 2) & (lane == width - 1) | (row == 3) & (lane == width - 2)
    return hit.astype(F32).astype(BF16)


def coefficients(we, wn, d):
    pe, ne = jnp.maximum(we, 0.0), jnp.minimum(we, 0.0)
    pn, nn = jnp.maximum(wn, 0.0), jnp.minimum(wn, 0.0)
    return 1.0 - pe + ne - pn + nn - 4.0 * d, pe + d, d - ne, pn + d, d - nn


def edge_kernel(rows, slots, me_ref, owner_ref, *refs):
    homes, (up_ref, down_ref, side_ref, rate_ref, in_ref) = refs[:8], refs[8:13]
    x_ref, halo_ref, block, taken, *tables, sems = refs[13:]
    held = [x_ref, *(rate_ref.at[j] for j in range(3)), halo_ref, *tables]
    copies = [pltpu.make_async_copy(a, b, sems.at[k]) for k, (a, b) in enumerate(zip(homes, held))]
    for copy in copies:
        copy.start()
    for copy in copies[1:]:
        copy.wait()
    sort_blocks(slots, me_ref[0], owner_ref, tables, in_ref, taken)
    copies[0].wait()
    wanted = halo_ref.shape[1]
    count = x_ref.shape[0] // rows
    width = x_ref.shape[1]

    def row(r):
        return x_ref[pl.ds(r, count, stride=rows), :].astype(BF16)

    for out_ref, near, far, q in ((up_ref, rows - 1, rows - 2, 1), (down_ref, 0, 1, 0)):
        out_ref[0:count, :] = row(near)
        out_ref[count : 2 * count, :] = row(far)
        block[...] = jnp.zeros(block.shape, F32)
        for j in range(3):
            hi, lo = split(rate_ref[j, near : near + 1, :])
            block[j : j + 1, :] = hi
            block[j + 3 : j + 4, :] = lo
        block[6:7, 0:wanted] = halo_ref[q : q + 1, :].astype(F32)
        out_ref[2 * count : 2 * count + 16, :] = block[...].astype(BF16)
    lane = iota((rows, count), 1)
    for i, (c, q) in enumerate(((width - 1, 3), (0, 2))):
        side_ref[i, 2 * rows : 3 * rows, :] = jnp.zeros((rows, count), F32)
        side_ref[i, 2 * rows + 2 : 2 * rows + 3, 0:wanted] = halo_ref[q : q + 1, :].astype(F32)
        rates = jnp.zeros((rows, count), F32)
        for j in range(3):
            hi, lo = split(rate_ref[j][:, c : c + 1])
            rates = jnp.where(lane == j, hi, jnp.where(lane == j + 3, lo, rates))
        side_ref[i, 3 * rows : 4 * rows, :] = rates
    pick = pick_columns(width)
    for r in range(rows):
        got = dot(pick, row(r), 1, 1)
        for i, k in enumerate((2, 0)):
            side_ref[i, r : r + 1, :] = got[k : k + 1, :]
            side_ref[i, rows + r : rows + r + 1, :] = got[k + 1 : k + 2, :]


def side_kernel(rows, south_ref, north_ref, side_ref, east_ref, west_ref):
    count, width = side_ref.shape[2], south_ref.shape[1]
    pick = pick_columns(width)
    south = dot(pick, south_ref[0:count, :], 1, 1)
    north = dot(pick, north_ref[0:count, :], 1, 1)
    line = iota((4 * rows, count), 0)
    for i, (out_ref, k) in enumerate(((east_ref, 2), (west_ref, 0))):
        v = jnp.where(line == 2 * rows, south[k : k + 1, :], side_ref[i])
        out_ref[...] = jnp.where(line == 2 * rows + 1, north[k : k + 1, :], v).astype(BF16)


def slot_of(owner, me, slots):
    if slots & (slots - 1):
        return lax.rem(owner - me + slots, slots)
    return lax.bitwise_xor(owner, me)


def sort_blocks(slots, me, owner_ref, lists, hold, taken):
    cap = hold.shape[1] // 3
    hold[...] = jnp.zeros(hold.shape, F32)
    for s in range(slots):
        taken[s] = 0

    @pl.loop(0, lists[0].shape[0])
    def _(b):
        s = slot_of(owner_ref[b], me, slots)
        at = jnp.minimum(taken[s], cap - 1)
        taken[s] = at + 1
        for k in range(3):
            hold[s, pl.ds(k * cap + at, 1), :] = lists[k][pl.ds(b, 1), :].astype(F32)


def sort_kernel(slots, me_ref, owner_ref, *refs):
    out_refs, (hold, taken) = refs[3 : 3 + slots], refs[3 + slots :]
    sort_blocks(slots, me_ref[0], owner_ref, refs[:3], hold, taken)
    for s in range(slots):
        out_refs[s][...] = hold[s]


def build_kernel(slots, *refs):
    list_refs, (out_ref, hot, spread) = refs[:-3], refs[-3:]
    nodes, cells = out_ref.shape[1], out_ref.shape[2]
    if len(list_refs) < slots:
        list_refs = [list_refs[0].at[s] for s in range(slots)]
    cap, entries = list_refs[0].shape[0] // 3, list_refs[0].shape[1]
    node_ids = iota((nodes, entries), 0).astype(F32)
    cell_ids = iota((entries, cells), 1).astype(F32)
    for s in range(slots):
        ref = list_refs[s]
        columns = ref[...].T
        for c in range(cap):
            lanes = slice(c * entries, (c + 1) * entries)
            cell, weight = (columns[:, k * cap + c : k * cap + c + 1] for k in (1, 2))
            hot[:, lanes] = jnp.where(node_ids == ref[c : c + 1, :], 1.0, 0.0).astype(BF16)
            spread[lanes, :] = jnp.where(cell_ids == cell, weight, 0.0).astype(BF16)
        out_ref[s] = dot(hot[...], spread[...]).astype(BF16)


def build(slots, nodes, cells, lists):
    cap, entries = lists[0].shape[-2] // 3, lists[0].shape[-1]
    size = slots * nodes * cells
    return call(
        functools.partial(build_kernel, slots),
        shape((slots, nodes, cells), BF16),
        lists,
        scratch=[pltpu.VMEM((nodes, cap * entries), BF16), pltpu.VMEM((cap * entries, cells), BF16)],
        vmem=8 + 3 * size // MIB,
        cost=cost(2 * size * cap * entries, 4 * size),
    )


def mend(rows, lat, lat_ref, c0, cw, ce, cs, cn):
    line = iota(c0.shape, 0)
    ps = jnp.where((line == 0) & (lat_ref[0] == 0), 1.0, 0.0)
    pn = jnp.where((line == rows - 1) & (lat_ref[0] == lat - 1), 1.0, 0.0)
    return c0 + ps * cs + pn * cn, cw, ce, cs * (1.0 - ps), cn * (1.0 - pn)


def turning(width):
    k, col = iota((2 * width, 2 * width), 0), iota((2 * width, 2 * width), 1)
    k = jnp.where(k < width, k, k - width)
    return jnp.where(jnp.where(col < width, col - 1, col - width + 1) == k, 1.0, 0.0).astype(BF16)


def advance(turn, rates, v, below, above):
    width = v.shape[1]
    hi = v.astype(BF16)
    turned = dot(jnp.concatenate([hi, (v - hi.astype(F32)).astype(BF16)], 1), turn)
    c0, cw, ce, cs, cn = rates
    return c0 * v + cw * turned[:, 0:width] + ce * turned[:, width : 2 * width] + cs * below + cn * above


def inner_kernel(rows, lat, lat_ref, x_ref, wind_ref, south_ref, north_ref, mid_ref, rate):
    count, width = mid_ref.shape[1], x_ref.shape[1]
    own = mend(rows, lat, lat_ref, *coefficients(wind_ref[0], wind_ref[1], wind_ref[2]))
    outer = []
    for ref in (south_ref, north_ref):
        v = ref[2 * count : 2 * count + 16, :].astype(F32)
        outer.append(coefficients(*(v[j : j + 1, :] + v[j + 3 : j + 4, :] for j in range(3))))
    for j in range(5):
        rate[j, 0:1, :] = outer[0][j]
        rate[j, 1 : rows + 1, :] = own[j]
        rate[j, rows + 1 : rows + 2, :] = outer[1][j]
    turn = turning(width)

    def cell_row(r):
        if r < 0:
            return south_ref[(-1 - r) * count : -r * count, :].astype(F32)
        if r >= rows:
            return north_ref[(r - rows) * count : (r - rows + 1) * count, :].astype(F32)
        return x_ref[pl.ds(r, count, stride=rows), :]

    for r in range(-1, rows + 1):
        rates = [rate[j, r + 1 : r + 2, :] for j in range(5)]
        mid_ref[r + 1] = advance(turn, rates, cell_row(r), cell_row(r - 1), cell_row(r + 1))


def step_kernel(rows, lat, slots, lat_ref, mid_ref, rate, side_ref, west_ref, east_ref, a_ref, u_ref, *rest):
    part_refs, (ring, b1, b2, mid, flat) = rest[:slots], rest[slots:]
    count, width = side_ref.shape[2], mid_ref.shape[2]
    west, east = west_ref[...].astype(F32), east_ref[...].astype(F32)
    w1, w2, w_corner, w_rate = (west[k * rows : (k + 1) * rows, :] for k in range(4))
    e1, e2, e_corner, e_rate = (east[k * rows : (k + 1) * rows, :] for k in range(4))
    half = ring.shape[0] // 2

    def place(out_ref, lines):
        k, col = iota((2 * half, lines * width), 0), iota((2 * half, lines * width), 1)
        hit = jnp.where(k < half, k * width, (k - half) * width + width - 1) == col
        out_ref[...] = dot(ring[...].astype(BF16), jnp.where(hit, 1.0, 0.0).astype(BF16), 0, 0)

    ring[...] = jnp.zeros(ring.shape, F32)
    for base, corner, near, j, c in ((0, w_corner, w1, 1, 0), (half, e_corner, e1, 2, width - 1)):
        k = rate[j, :, c : c + 1]
        ring[base : base + 1, :] = k[0:1, :] * corner[0:1, :]
        ring[base + 1 : base + 1 + rows, :] = k[1 : rows + 1, :] * near
        ring[base + 1 + rows : base + 2 + rows, :] = k[rows + 1 : rows + 2, :] * corner[1:2, :]
    place(b1, rows + 2)

    def ring_col(rates, corner, v, out_w, out_e):
        rates = coefficients(*(rates[:, j : j + 1] + rates[:, j + 3 : j + 4] for j in range(3)))
        k0, kw, ke, ks, kn = mend(rows, lat, lat_ref, *rates)
        line = iota(v.shape, 0)
        to_s = jnp.where(line == 0, corner[0:1, :], pltpu.roll(v, 1, 0))
        to_n = jnp.where(line == rows - 1, corner[1:2, :], pltpu.roll(v, rows - 1, 0))
        return k0 * v + kw * out_w + ke * out_e + ks * to_s + kn * to_n

    ring[...] = jnp.zeros(ring.shape, F32)
    kw, ke = rate[1, 1 : rows + 1, 0:1], rate[2, 1 : rows + 1, width - 1 : width]
    ring[0:rows, :] = kw * ring_col(w_rate, w_corner, w1, w2, side_ref[1, 0:rows, :])
    ring[half : half + rows, :] = ke * ring_col(e_rate, e_corner, e1, side_ref[0, 0:rows, :], e2)
    place(b2, rows)

    for r in range(rows + 2):
        mid[r] = mid_ref[r] + b1[:, r * width : (r + 1) * width]
    turn = turning(width)
    for r in range(rows):
        here = slice(r * width, (r + 1) * width)
        rates = [rate[j, r + 1 : r + 2, :] for j in range(5)]
        new = advance(turn, rates, mid[r + 1], mid[r], mid[r + 2]) + b2[:, here]
        u_ref[:, here] = new
        flat[:, here] = new.astype(BF16)
    for s in range(slots):
        part_refs[s][...] = dot(a_ref[s], flat[...], 1, 1).astype(part_refs[s].dtype)


def silu(v):
    return 0.5 * v * (1.0 + jnp.tanh(0.5 * v))


def normalize(v):
    return (v * lax.rsqrt(jnp.mean(v * v, axis=-1, keepdims=True) + 1e-06)).astype(BF16)


def link_kernel(sender_ref, receiver_ref, gather_ref, scatter_ref, local_ref, order):
    edges, known = gather_ref.shape
    nodes = scatter_ref.shape[0]
    sender, receiver = sender_ref[...], receiver_ref[...]
    local = jnp.where(sender < nodes, 1.0, 0.0)
    order[...] = jnp.where(iota((edges, edges), 0) < iota((edges, edges), 1), 1.0, 0.0).astype(BF16)
    before = dot(jnp.broadcast_to(local, (16, edges)).astype(BF16), order[...])[0:1, :]
    total = jnp.sum(local)
    local_ref[0] = total.astype(I32)
    index = iota((1, edges), 1).astype(F32)
    place = jnp.where(sender < nodes, before, total + index - before)
    order[...] = jnp.where(iota((edges, edges), 0).astype(F32) == place, 1.0, 0.0).astype(BF16)
    line = iota((16, edges), 0)
    high = sender // nodes
    keys = jnp.where(line == 0, sender - high * nodes, jnp.where(line == 1, high, jnp.where(line == 2, receiver, 0)))
    keys = keys.astype(F32).astype(BF16)
    cols = dot(order[...], keys, 1, 1)
    sender, receiver = cols[:, 0:1] + nodes * cols[:, 1:2], cols[:, 2:3]
    lane = iota((edges, nodes), 1).astype(F32)
    gather_ref[:, 0:nodes] = jnp.where(sender == lane, 1.0, 0.0).astype(BF16)
    gather_ref[:, nodes : 2 * nodes] = jnp.where(receiver == lane, 1.0, 0.0).astype(BF16)
    rest = (iota((edges, known - 2 * nodes), 1) + nodes).astype(F32)
    gather_ref[:, 2 * nodes :] = jnp.where(sender == rest, 1.0, 0.0).astype(BF16)
    row = dot(keys, order[...], 1, 1)[2:3, :]
    scatter_ref[...] = jnp.where(row == iota((nodes, edges), 0).astype(F32), 1.0, 0.0).astype(BF16)


def project(m, hidden, owed, ws, wr, table_ref, out_refs, wanted, nodes):
    normed = normalize(hidden)
    source = dot(normed, ws).astype(BF16)
    table_ref[m, 0:nodes, :] = source
    table_ref[m, nodes : 2 * nodes, :] = dot(normed, wr).astype(BF16)
    for q in range(4):
        out_refs[q][m * wanted : (m + 1) * wanted, :] = dot(owed[q], source).astype(BF16)


def owed_kernel(rows, wanted, south_ref, north_ref, west_ref, east_ref, enc_ref, owed_ref, pad_ref):
    nodes = owed_ref.shape[1]
    count = west_ref.shape[1]
    lists = [ref[2 * count : 2 * count + 16, :].astype(F32)[6:7, :] for ref in (south_ref, north_ref)]
    lists += [ref[2 * rows : 4 * rows, 0:128].astype(F32)[2:3, :] for ref in (west_ref, east_ref)]
    for q in range(4):
        hot = jnp.where(iota((nodes, 128), 0).astype(F32) == lists[q], 1.0, 0.0)
        owed_ref[q * wanted : (q + 1) * wanted, :] = hot.T[0:wanted, :].astype(BF16)
    quantities = enc_ref.shape[0]
    pad_ref[...] = jnp.zeros(pad_ref.shape, BF16)
    for m in range(pad_ref.shape[0]):
        pad_ref[m, m * quantities : (m + 1) * quantities, :] = enc_ref[...]


def encode_kernel(slots, wanted, *refs):
    part_refs = refs[:slots]
    pad_ref, ws_ref, wr_ref, owed_ref, hidden_ref, table_ref, *out_refs = refs[slots:]
    nodes = part_refs[0].shape[0]
    owed = [owed_ref[q * wanted : (q + 1) * wanted, :] for q in range(4)]
    total = part_refs[0][...].astype(F32)
    for ref in part_refs[1:]:
        total = total + ref[...].astype(F32)
    total = total.astype(BF16)
    for m in range(hidden_ref.shape[0]):
        hidden = silu(dot(total, pad_ref[m]))
        hidden_ref[m] = hidden
        project(m, hidden, owed, ws_ref[0], wr_ref[0], table_ref, out_refs, wanted, nodes)


def pieces(chunk):
    step = chunk // 3
    return [(k, step) for k in range(0, chunk, step)]


def early_kernel(chunk, local_ref, table_ref, gather_ref, scatter_ref, sums_ref, terms_ref):
    members, depth, _ = table_ref.shape
    edges = gather_ref.shape[0]
    sums_ref[...] = jnp.zeros(sums_ref.shape, F32)

    @pl.loop(0, edges // chunk)
    def _(c):
        at = pl.multiple_of(c * chunk, chunk)
        here = c < local_ref[0] // chunk

        @pl.when(here)
        def _():
            for m in range(members):
                found = [
                    silu(dot(gather_ref[pl.ds(at + k, n), 0:depth], table_ref[m])).astype(BF16)
                    for k, n in pieces(chunk)
                ]
                sums_ref[m] += dot(scatter_ref[:, pl.ds(at, chunk)], jnp.concatenate(found, 0))

        @pl.when(jnp.logical_not(here))
        def _():
            for m in range(members):
                for k, n in pieces(chunk):
                    terms_ref[m, pl.ds(at + k, n), :] = dot(gather_ref[pl.ds(at + k, n), 0:depth], table_ref[m])


def late_messages(chunk, local_ref, gather_ref, scatter_ref, depth, terms_ref, known, chosen, sums_ref):
    edges = gather_ref.shape[0]

    @pl.loop(local_ref[0] // chunk, edges // chunk)
    def _(c):
        at = pl.multiple_of(c * chunk, chunk)
        for m in chosen:
            found = []
            for k, n in pieces(chunk):
                v = terms_ref[m, pl.ds(at + k, n), :] + dot(gather_ref[pl.ds(at + k, n), depth:], known[m])
                found.append(silu(v).astype(BF16))
            sums_ref[m] += dot(scatter_ref[:, pl.ds(at, chunk)], jnp.concatenate(found, 0))


def layer_kernel(layer, only, wanted, chunk, *refs):
    local_ref, hidden_ref, terms_ref, owed_ref, gather_ref, scatter_ref, early_ref = refs[:7]
    halo_refs, wu_ref = refs[7:11], refs[11]
    last = only is not None
    if last:
        dec_ref, out_ref, known, sums = refs[12:]
    else:
        ws_ref, wr_ref, next_hidden_ref, next_table_ref, *out_refs, known, sums = refs[12:]
    members, nodes, width = hidden_ref.shape
    chosen = (only,) if last else range(members)
    for m in chosen:
        sums[m] = early_ref[m]
        for q in range(4):
            known[m, q * wanted : (q + 1) * wanted, :] = halo_refs[q][m * wanted : (m + 1) * wanted, :]
        known[m, 4 * wanted :, :] = jnp.zeros((known.shape[1] - 4 * wanted, width), BF16)
    late_messages(chunk, local_ref, gather_ref, scatter_ref, 2 * nodes, terms_ref, known, chosen, sums)
    if not last:
        owed = [owed_ref[q * wanted : (q + 1) * wanted, :] for q in range(4)]
    for m in chosen:
        hidden = hidden_ref[m] + dot(sums[m].astype(BF16), wu_ref[layer])
        if last:
            out_ref[...] = dot(dec_ref[...], normalize(hidden), 1, 1).astype(BF16)
        else:
            next_hidden_ref[m] = hidden
            project(m, hidden, owed, ws_ref[layer + 1], wr_ref[layer + 1], next_table_ref, out_refs, wanted, nodes)


def land_kernel(rows, slots, member, u_ref, w_ref, *refs):
    corr_refs, (out_ref, tile, sem) = refs[:slots], refs[-3:]
    quantities, width = corr_refs[0].shape[0], u_ref.shape[1] // rows
    total = u_ref[member * quantities : (member + 1) * quantities, :]
    for s in range(slots):
        total = total + dot(corr_refs[s][...], w_ref[s])
    for r in range(rows):
        tile[pl.ds(r, quantities, stride=rows), :] = total[:, r * width : (r + 1) * width]
    size = quantities * rows
    copy = pltpu.make_async_copy(tile, out_ref.at[member * size : (member + 1) * size], sem)
    copy.start()
    copy.wait()


def land(kernel, x, args, onward, size, lon):
    spaces = [pl.BlockSpec(memory_space=pltpu.VMEM)] * (len(args) - onward)
    spaces += [pl.BlockSpec(memory_space=pl.ANY)] * onward
    return pl.pallas_call(
        kernel,
        out_shape=shape(x.shape, F32),
        in_specs=spaces,
        out_specs=pl.BlockSpec(memory_space=pl.ANY),
        scratch_shapes=[pltpu.VMEM((size, x.shape[1]), F32), pltpu.SemaphoreType.DMA],
        input_output_aliases={len(args) - 1: 0} if onward else {},
        compiler_params=pltpu.CompilerParams(vmem_limit_bytes=(16 + lon) * MIB),
        cost_estimate=cost(1e9, 6 * MIB),
    )(*args)


def body(
    fields, wind_east, wind_north, diffusion, inflow_owner, inflow_cell, inflow_node, inflow_weight,
    encoder, sender_weight, receiver_weight, update_weight, decoder, edge_sender, edge_receiver, halo_rows,
    outflow_owner, outflow_node, outflow_cell, outflow_weight,
):
    members, quantities, rows, width = fields.shape
    count, cells = members * quantities, rows * width
    lon, lat = lax.axis_size("lon"), lax.axis_size("lat")
    me = lax.axis_index("lon").astype(I32).reshape(1)
    lat_at = lax.axis_index("lat").astype(I32).reshape(1)
    blocks, entries = inflow_cell.shape
    hid = encoder.shape[1]
    layers = sender_weight.shape[0]
    edges = edge_sender.shape[-1]
    wanted = halo_rows.shape[-1]
    nodes = NODE_DEV
    cap = max(2, -(-2 * blocks // lon))

    def shift(v, s):
        return lax.ppermute(v, "lon", [(i, (i + s) % lon) for i in range(lon)])

    def peer(v, s):
        if lon & (lon - 1):
            return shift(v, s)
        return lax.ppermute(v, "lon", [(i, i ^ s) for i in range(lon)])

    def up(v):
        return lax.ppermute(v, "lat", [(i, (i + 1) % lat) for i in range(lat)])

    def down(v):
        return lax.ppermute(v, "lat", [((i + 1) % lat, i) for i in range(lat)])

    x = fields.reshape(count * rows, width)
    halo = halo_rows.reshape(4, wanted)
    rates = (wind_east, wind_north, diffusion)
    tall = 2 * count + 16
    tables = (inflow_node, inflow_cell, inflow_weight)
    taken = pltpu.SMEM((lon,), I32)
    to_north, to_south, side, wind, in_lists = call(
        functools.partial(edge_kernel, rows, lon),
        [shape((tall, width), BF16), shape((tall, width), BF16), shape((2, 4 * rows, count), F32),
         shape((3, rows, width), F32), shape((lon, 3 * cap, entries), F32)],
        (me, inflow_owner.reshape(blocks), x, *rates, halo, *tables),
        smem=2,
        away=8,
        scratch=[
            pltpu.VMEM(x.shape, F32),
            pltpu.VMEM(halo.shape, I32),
            pltpu.VMEM((16, width), F32),
            taken,
            *(pltpu.VMEM(v.shape, v.dtype) for v in tables),
            pltpu.SemaphoreType.DMA((8,)),
        ],
        vmem=56,
        cost=cost(0, 8 * MIB),
    )
    south, north = up(to_north), down(to_south)
    into = build(lon, nodes, cells, (in_lists,))
    side, into = lax.optimization_barrier((side, into))
    to_east, to_west = call(
        functools.partial(side_kernel, rows),
        (shape((4 * rows, count), BF16), shape((4 * rows, count), BF16)),
        (south, north, side),
        vmem=4,
        cost=cost(0, 4 * MIB),
    )
    west, east = shift(to_east, 1), shift(to_west, lon - 1)

    x, _ = lax.optimization_barrier((x, to_east))
    mid, rate = call(
        functools.partial(inner_kernel, rows, lat),
        (shape((rows + 2, count, width), F32), shape((5, rows + 2, width), F32)),
        (lat_at, x, wind, south, north),
        smem=1,
        vmem=12,
        cost=cost(1e9, 6 * MIB),
    )
    u, *parts = call(
        functools.partial(step_kernel, rows, lat, lon),
        [shape((count, cells), F32)] + [shape((nodes, count), F32)] + [shape((nodes, count), BF16)] * (lon - 1),
        (lat_at, mid, rate, side, west, east, into),
        smem=1,
        scratch=[
            pltpu.VMEM((32, count), F32),
            pltpu.VMEM((count, (rows + 2) * width), F32),
            pltpu.VMEM((count, cells), F32),
            pltpu.VMEM((rows + 2, count, width), F32),
            pltpu.VMEM((count, cells), BF16),
        ],
        vmem=14 + lon * 2,
        cost=cost(2 * lon * nodes * cells * count, 16 * MIB),
    )
    parts, edge_sender, edge_receiver, outflow_node = lax.optimization_barrier(
        (parts, edge_sender, edge_receiver, outflow_node)
    )
    got = [peer(parts[s], s) for s in range(lon - 1, 0, -1)]
    parts = parts[:1] + got[::-1]

    known = 2 * nodes + 256 * -(-4 * wanted // 256)
    chunk = edges // 2
    gather, scatter, local = call(
        link_kernel,
        (shape((edges, known), BF16), shape((nodes, edges), BF16), shape((1,), I32)),
        (edge_sender.reshape(1, edges), edge_receiver.reshape(1, edges)),
        small=1,
        scratch=[pltpu.VMEM((edges, edges), BF16)],
        vmem=24,
        cost=cost(2 * edges * edges * 48, 8 * MIB),
    )
    out_lists = call(
        functools.partial(sort_kernel, lon),
        [shape((3 * cap, entries), F32)] * lon,
        (me, outflow_owner.reshape(blocks), outflow_node, outflow_cell, outflow_weight),
        smem=2,
        scratch=[pltpu.VMEM((lon, 3 * cap, entries), F32), taken],
        vmem=4,
        cost=cost(0, MIB),
    )
    scatter, out_lists = lax.optimization_barrier((scatter, out_lists))
    out_lists = [out_lists[0]] + [peer(out_lists[s], s) for s in range(1, lon)]
    parts, out_lists = lax.optimization_barrier((parts, out_lists))
    onto = build(lon, nodes, cells, out_lists)

    reply = [shape((members * wanted, hid), BF16)] * 4
    state = [shape((members, nodes, hid), F32), shape((members, 2 * nodes, hid), BF16)]
    owed, pad = call(
        functools.partial(owed_kernel, rows, wanted),
        (shape((4 * wanted, nodes), BF16), shape((members, count, hid), BF16)),
        (south, north, west, east, encoder),
        vmem=8,
        cost=cost(0, 4 * MIB),
    )
    hidden, table, *out = call(
        functools.partial(encode_kernel, lon, wanted),
        state + reply,
        (*parts, pad, sender_weight, receiver_weight, owed),
        vmem=16,
        cost=cost(2e9, 8 * MIB),
    )
    for layer in range(layers):
        halos = [shift(out[3], 1), shift(out[2], lon - 1), up(out[1]), down(out[0])]
        halos = halos[2:] + halos[:2]
        early, terms = call(
            functools.partial(early_kernel, chunk),
            (shape((members, nodes, hid), F32), shape((members, edges, hid), F32)),
            (local, table, gather, scatter),
            smem=1,
            vmem=16,
            cost=cost(3e9, 8 * MIB),
        )
        last = layer == layers - 1
        args = (local, hidden, terms, owed, gather, scatter, early, *halos, update_weight)
        scratch = [pltpu.VMEM((members, known - 2 * nodes, hid), BF16), pltpu.VMEM((members, nodes, hid), F32)]
        if last:
            corrs = [
                call(
                    functools.partial(layer_kernel, layer, m, wanted, chunk), shape((quantities, nodes), BF16),
                    (*args, decoder.T), smem=1, scratch=scratch, vmem=20, cost=cost(2e9, 8 * MIB),
                )
                for m in range(members)
            ]
        else:
            hidden, table, *out = call(
                functools.partial(layer_kernel, layer, None, wanted, chunk),
                state + reply,
                (*args, sender_weight, receiver_weight),
                smem=1,
                scratch=scratch,
                vmem=20,
                cost=cost(4e9, 12 * MIB),
            )
    corrs = [[v] + [peer(v, s) for s in range(lon - 1, 0, -1)] for v in corrs]
    out = None
    for m in range(members):
        got = [corrs[m][0]] + corrs[m][:0:-1]
        args = (u, onto, *got) if out is None else (u, onto, *got, out)
        out = land(functools.partial(land_kernel, rows, lon, m), x, args, out is not None, rows * quantities, lon)
    return out.reshape(members, quantities, rows, width)


def solution(mesh):
    tile, block, part = P("lat", "lon"), P(("lat", "lon"), None), P("lat", "lon", None)
    placed = (P("member", None, "lat", "lon"), tile, tile, tile, block, block, block, block)
    placed += (P(),) * 5 + (part, part, P("lat", "lon", None, None)) + (block,) * 4
    return jax.shard_map(
        body, mesh=mesh, in_specs=placed, out_specs=P("member", None, "lat", "lon"), check_vma=False
    )
```

```python
import functools

import jax
import jax.numpy as jnp
from jax import lax
from jax.experimental import pallas as pl
from jax.experimental.pallas import tpu as pltpu
from jax.sharding import PartitionSpec as P

F32, BF16, I32 = jnp.float32, jnp.bfloat16, jnp.int32
MIB = 1 << 20
SCALE = 0.05
NODE_DEV = 256


def dot(a, b, ca=1, cb=0):
    return lax.dot_general(a, b, (((ca,), (cb,)), ((), ())), preferred_element_type=F32)


def iota(shape, dim):
    return lax.broadcasted_iota(I32, shape, dim)


def call(kernel, outs, args, smem=0, away=0, small=0, scratch=(), vmem=32, cost=None):
    single = not isinstance(outs, (list, tuple))
    spaces = [pltpu.SMEM] * smem + [pl.ANY] * away + [pltpu.VMEM] * (len(args) - smem - away)
    if single:
        out_specs = pl.BlockSpec(memory_space=pltpu.VMEM)
    else:
        homes = [pltpu.VMEM] * (len(outs) - small) + [pltpu.SMEM] * small
        out_specs = tuple(pl.BlockSpec(memory_space=m) for m in homes)
    return pl.pallas_call(
        kernel,
        out_shape=outs if single else tuple(outs),
        in_specs=[pl.BlockSpec(memory_space=m) for m in spaces],
        out_specs=out_specs,
        scratch_shapes=list(scratch),
        compiler_params=pltpu.CompilerParams(vmem_limit_bytes=vmem * MIB),
        cost_estimate=cost,
    )(*args)


def cost(flops, bytes_accessed):
    return pl.CostEstimate(flops=int(flops * SCALE), bytes_accessed=int(bytes_accessed * SCALE), transcendentals=0)


def shape(dims, dtype):
    return jax.ShapeDtypeStruct(tuple(dims), dtype)


def split(v):
    hi = v.astype(BF16).astype(F32)
    return hi, v - hi


def pick_columns(width):
    row, lane = iota((16, width), 0), iota((16, width), 1)
    hit = (row == 0) & (lane == 0) | (row == 1) & (lane == 1)
    hit = hit | (row == 2) & (lane == width - 1) | (row == 3) & (lane == width - 2)
    return hit.astype(F32).astype(BF16)


def coefficients(we, wn, d):
    pe, ne = jnp.maximum(we, 0.0), jnp.minimum(we, 0.0)
    pn, nn = jnp.maximum(wn, 0.0), jnp.minimum(wn, 0.0)
    return 1.0 - pe + ne - pn + nn - 4.0 * d, pe + d, d - ne, pn + d, d - nn


def edge_kernel(rows, slots, me_ref, owner_ref, *refs):
    homes, (up_ref, down_ref, side_ref, rate_ref, in_ref) = refs[:8], refs[8:13]
    x_ref, halo_ref, block, taken, *tables, sems = refs[13:]
    held = [x_ref, *(rate_ref.at[j] for j in range(3)), halo_ref, *tables]
    copies = [pltpu.make_async_copy(a, b, sems.at[k]) for k, (a, b) in enumerate(zip(homes, held))]
    for copy in copies:
        copy.start()
    for copy in copies[1:]:
        copy.wait()
    sort_blocks(slots, me_ref[0], owner_ref, tables, in_ref, taken)
    copies[0].wait()
    wanted = halo_ref.shape[1]
    count = x_ref.shape[0] // rows
    width = x_ref.shape[1]

    def row(r):
        return x_ref[pl.ds(r, count, stride=rows), :].astype(BF16)

    for out_ref, near, far, q in ((up_ref, rows - 1, rows - 2, 1), (down_ref, 0, 1, 0)):
        out_ref[0:count, :] = row(near)
        out_ref[count : 2 * count, :] = row(far)
        block[...] = jnp.zeros(block.shape, F32)
        for j in range(3):
            hi, lo = split(rate_ref[j, near : near + 1, :])
            block[j : j + 1, :] = hi
            block[j + 3 : j + 4, :] = lo
        block[6:7, 0:wanted] = halo_ref[q : q + 1, :].astype(F32)
        out_ref[2 * count : 2 * count + 16, :] = block[...].astype(BF16)
    lane = iota((rows, count), 1)
    for i, (c, q) in enumerate(((width - 1, 3), (0, 2))):
        side_ref[i, 2 * rows : 3 * rows, :] = jnp.zeros((rows, count), F32)
        side_ref[i, 2 * rows + 2 : 2 * rows + 3, 0:wanted] = halo_ref[q : q + 1, :].astype(F32)
        rates = jnp.zeros((rows, count), F32)
        for j in range(3):
            hi, lo = split(rate_ref[j][:, c : c + 1])
            rates = jnp.where(lane == j, hi, jnp.where(lane == j + 3, lo, rates))
        side_ref[i, 3 * rows : 4 * rows, :] = rates
    pick = pick_columns(width)
    for r in range(rows):
        got = dot(pick, row(r), 1, 1)
        for i, k in enumerate((2, 0)):
            side_ref[i, r : r + 1, :] = got[k : k + 1, :]
            side_ref[i, rows + r : rows + r + 1, :] = got[k + 1 : k + 2, :]


def side_kernel(rows, south_ref, north_ref, side_ref, east_ref, west_ref):
    count, width = side_ref.shape[2], south_ref.shape[1]
    pick = pick_columns(width)
    south = dot(pick, south_ref[0:count, :], 1, 1)
    north = dot(pick, north_ref[0:count, :], 1, 1)
    line = iota((4 * rows, count), 0)
    for i, (out_ref, k) in enumerate(((east_ref, 2), (west_ref, 0))):
        v = jnp.where(line == 2 * rows, south[k : k + 1, :], side_ref[i])
        out_ref[...] = jnp.where(line == 2 * rows + 1, north[k : k + 1, :], v).astype(BF16)


def slot_of(owner, me, slots):
    if slots & (slots - 1):
        return lax.rem(owner - me + slots, slots)
    return lax.bitwise_xor(owner, me)


def sort_blocks(slots, me, owner_ref, lists, hold, taken):
    cap = hold.shape[1] // 3
    hold[...] = jnp.zeros(hold.shape, F32)
    for s in range(slots):
        taken[s] = 0

    @pl.loop(0, lists[0].shape[0])
    def _(b):
        s = slot_of(owner_ref[b], me, slots)
        at = jnp.minimum(taken[s], cap - 1)
        taken[s] = at + 1
        for k in range(3):
            hold[s, pl.ds(k * cap + at, 1), :] = lists[k][pl.ds(b, 1), :].astype(F32)


def sort_kernel(slots, me_ref, owner_ref, *refs):
    out_refs, (hold, taken) = refs[3 : 3 + slots], refs[3 + slots :]
    sort_blocks(slots, me_ref[0], owner_ref, refs[:3], hold, taken)
    for s in range(slots):
        out_refs[s][...] = hold[s]


def build_kernel(slots, *refs):
    list_refs, (out_ref, hot, spread) = refs[:-3], refs[-3:]
    nodes, cells = out_ref.shape[1], out_ref.shape[2]
    if len(list_refs) < slots:
        list_refs = [list_refs[0].at[s] for s in range(slots)]
    cap, entries = list_refs[0].shape[0] // 3, list_refs[0].shape[1]
    node_ids = iota((nodes, entries), 0).astype(F32)
    cell_ids = iota((entries, cells), 1).astype(F32)
    for s in range(slots):
        ref = list_refs[s]
        columns = ref[...].T
        for c in range(cap):
            lanes = slice(c * entries, (c + 1) * entries)
            cell, weight = (columns[:, k * cap + c : k * cap + c + 1] for k in (1, 2))
            hot[:, lanes] = jnp.where(node_ids == ref[c : c + 1, :], 1.0, 0.0).astype(BF16)
            spread[lanes, :] = jnp.where(cell_ids == cell, weight, 0.0).astype(BF16)
        out_ref[s] = dot(hot[...], spread[...]).astype(BF16)


def build(slots, nodes, cells, lists):
    cap, entries = lists[0].shape[-2] // 3, lists[0].shape[-1]
    size = slots * nodes * cells
    return call(
        functools.partial(build_kernel, slots),
        shape((slots, nodes, cells), BF16),
        lists,
        scratch=[pltpu.VMEM((nodes, cap * entries), BF16), pltpu.VMEM((cap * entries, cells), BF16)],
        vmem=8 + 3 * size // MIB,
        cost=cost(2 * size * cap * entries, 4 * size),
    )


def mend(rows, lat, lat_ref, c0, cw, ce, cs, cn):
    line = iota(c0.shape, 0)
    ps = jnp.where((line == 0) & (lat_ref[0] == 0), 1.0, 0.0)
    pn = jnp.where((line == rows - 1) & (lat_ref[0] == lat - 1), 1.0, 0.0)
    return c0 + ps * cs + pn * cn, cw, ce, cs * (1.0 - ps), cn * (1.0 - pn)


def turning(width):
    k, col = iota((2 * width, 2 * width), 0), iota((2 * width, 2 * width), 1)
    k = jnp.where(k < width, k, k - width)
    return jnp.where(jnp.where(col < width, col - 1, col - width + 1) == k, 1.0, 0.0).astype(BF16)


def advance(turn, rates, v, below, above):
    width = v.shape[1]
    hi = v.astype(BF16)
    turned = dot(jnp.concatenate([hi, (v - hi.astype(F32)).astype(BF16)], 1), turn)
    c0, cw, ce, cs, cn = rates
    return c0 * v + cw * turned[:, 0:width] + ce * turned[:, width : 2 * width] + cs * below + cn * above


def inner_kernel(rows, lat, lat_ref, x_ref, wind_ref, south_ref, north_ref, mid_ref, rate):
    count, width = mid_ref.shape[1], x_ref.shape[1]
    own = mend(rows, lat, lat_ref, *coefficients(wind_ref[0], wind_ref[1], wind_ref[2]))
    outer = []
    for ref in (south_ref, north_ref):
        v = ref[2 * count : 2 * count + 16, :].astype(F32)
        outer.append(coefficients(*(v[j : j + 1, :] + v[j + 3 : j + 4, :] for j in range(3))))
    for j in range(5):
        rate[j, 0:1, :] = outer[0][j]
        rate[j, 1 : rows + 1, :] = own[j]
        rate[j, rows + 1 : rows + 2, :] = outer[1][j]
    turn = turning(width)

    def cell_row(r):
        if r < 0:
            return south_ref[(-1 - r) * count : -r * count, :].astype(F32)
        if r >= rows:
            return north_ref[(r - rows) * count : (r - rows + 1) * count, :].astype(F32)
        return x_ref[pl.ds(r, count, stride=rows), :]

    for r in range(-1, rows + 1):
        rates = [rate[j, r + 1 : r + 2, :] for j in range(5)]
        mid_ref[r + 1] = advance(turn, rates, cell_row(r), cell_row(r - 1), cell_row(r + 1))


def step_kernel(rows, lat, slots, lat_ref, mid_ref, rate, side_ref, west_ref, east_ref, a_ref, u_ref, *rest):
    part_refs, (ring, b1, b2, mid, flat) = rest[:slots], rest[slots:]
    count, width = side_ref.shape[2], mid_ref.shape[2]
    west, east = west_ref[...].astype(F32), east_ref[...].astype(F32)
    w1, w2, w_corner, w_rate = (west[k * rows : (k + 1) * rows, :] for k in range(4))
    e1, e2, e_corner, e_rate = (east[k * rows : (k + 1) * rows, :] for k in range(4))
    half = ring.shape[0] // 2

    def place(out_ref, lines):
        k, col = iota((2 * half, lines * width), 0), iota((2 * half, lines * width), 1)
        hit = jnp.where(k < half, k * width, (k - half) * width + width - 1) == col
        out_ref[...] = dot(ring[...].astype(BF16), jnp.where(hit, 1.0, 0.0).astype(BF16), 0, 0)

    ring[...] = jnp.zeros(ring.shape, F32)
    for base, corner, near, j, c in ((0, w_corner, w1, 1, 0), (half, e_corner, e1, 2, width - 1)):
        k = rate[j, :, c : c + 1]
        ring[base : base + 1, :] = k[0:1, :] * corner[0:1, :]
        ring[base + 1 : base + 1 + rows, :] = k[1 : rows + 1, :] * near
        ring[base + 1 + rows : base + 2 + rows, :] = k[rows + 1 : rows + 2, :] * corner[1:2, :]
    place(b1, rows + 2)

    def ring_col(rates, corner, v, out_w, out_e):
        rates = coefficients(*(rates[:, j : j + 1] + rates[:, j + 3 : j + 4] for j in range(3)))
        k0, kw, ke, ks, kn = mend(rows, lat, lat_ref, *rates)
        line = iota(v.shape, 0)
        to_s = jnp.where(line == 0, corner[0:1, :], pltpu.roll(v, 1, 0))
        to_n = jnp.where(line == rows - 1, corner[1:2, :], pltpu.roll(v, rows - 1, 0))
        return k0 * v + kw * out_w + ke * out_e + ks * to_s + kn * to_n

    ring[...] = jnp.zeros(ring.shape, F32)
    kw, ke = rate[1, 1 : rows + 1, 0:1], rate[2, 1 : rows + 1, width - 1 : width]
    ring[0:rows, :] = kw * ring_col(w_rate, w_corner, w1, w2, side_ref[1, 0:rows, :])
    ring[half : half + rows, :] = ke * ring_col(e_rate, e_corner, e1, side_ref[0, 0:rows, :], e2)
    place(b2, rows)

    for r in range(rows + 2):
        mid[r] = mid_ref[r] + b1[:, r * width : (r + 1) * width]
    turn = turning(width)
    for r in range(rows):
        here = slice(r * width, (r + 1) * width)
        rates = [rate[j, r + 1 : r + 2, :] for j in range(5)]
        new = advance(turn, rates, mid[r + 1], mid[r], mid[r + 2]) + b2[:, here]
        u_ref[:, here] = new
        flat[:, here] = new.astype(BF16)
    for s in range(slots):
        part_refs[s][...] = dot(a_ref[s], flat[...], 1, 1).astype(part_refs[s].dtype)


def silu(v):
    return 0.5 * v * (1.0 + jnp.tanh(0.5 * v))


def normalize(v):
    return (v * lax.rsqrt(jnp.mean(v * v, axis=-1, keepdims=True) + 1e-06)).astype(BF16)


def link_kernel(sender_ref, receiver_ref, gather_ref, scatter_ref, local_ref, order):
    edges, known = gather_ref.shape
    nodes = scatter_ref.shape[0]
    sender, receiver = sender_ref[...], receiver_ref[...]
    local = jnp.where(sender < nodes, 1.0, 0.0)
    order[...] = jnp.where(iota((edges, edges), 0) < iota((edges, edges), 1), 1.0, 0.0).astype(BF16)
    before = dot(jnp.broadcast_to(local, (16, edges)).astype(BF16), order[...])[0:1, :]
    total = jnp.sum(local)
    local_ref[0] = total.astype(I32)
    index = iota((1, edges), 1).astype(F32)
    place = jnp.where(sender < nodes, before, total + index - before)
    order[...] = jnp.where(iota((edges, edges), 0).astype(F32) == place, 1.0, 0.0).astype(BF16)
    line = iota((16, edges), 0)
    high = sender // nodes
    keys = jnp.where(line == 0, sender - high * nodes, jnp.where(line == 1, high, jnp.where(line == 2, receiver, 0)))
    keys = keys.astype(F32).astype(BF16)
    cols = dot(order[...], keys, 1, 1)
    sender, receiver = cols[:, 0:1] + nodes * cols[:, 1:2], cols[:, 2:3]
    lane = iota((edges, nodes), 1).astype(F32)
    gather_ref[:, 0:nodes] = jnp.where(sender == lane, 1.0, 0.0).astype(BF16)
    gather_ref[:, nodes : 2 * nodes] = jnp.where(receiver == lane, 1.0, 0.0).astype(BF16)
    rest = (iota((edges, known - 2 * nodes), 1) + nodes).astype(F32)
    gather_ref[:, 2 * nodes :] = jnp.where(sender == rest, 1.0, 0.0).astype(BF16)
    row = dot(keys, order[...], 1, 1)[2:3, :]
    scatter_ref[...] = jnp.where(row == iota((nodes, edges), 0).astype(F32), 1.0, 0.0).astype(BF16)


def project(m, hidden, owed, ws, wr, table_ref, out_refs, wanted, nodes):
    normed = normalize(hidden)
    source = dot(normed, ws).astype(BF16)
    table_ref[m, 0:nodes, :] = source
    table_ref[m, nodes : 2 * nodes, :] = dot(normed, wr).astype(BF16)
    for q in range(4):
        out_refs[q][m * wanted : (m + 1) * wanted, :] = dot(owed[q], source).astype(BF16)


def owed_kernel(rows, wanted, south_ref, north_ref, west_ref, east_ref, enc_ref, owed_ref, pad_ref):
    nodes = owed_ref.shape[1]
    count = west_ref.shape[1]
    lists = [ref[2 * count : 2 * count + 16, :].astype(F32)[6:7, :] for ref in (south_ref, north_ref)]
    lists += [ref[2 * rows : 4 * rows, 0:128].astype(F32)[2:3, :] for ref in (west_ref, east_ref)]
    for q in range(4):
        hot = jnp.where(iota((nodes, 128), 0).astype(F32) == lists[q], 1.0, 0.0)
        owed_ref[q * wanted : (q + 1) * wanted, :] = hot.T[0:wanted, :].astype(BF16)
    quantities = enc_ref.shape[0]
    pad_ref[...] = jnp.zeros(pad_ref.shape, BF16)
    for m in range(pad_ref.shape[0]):
        pad_ref[m, m * quantities : (m + 1) * quantities, :] = enc_ref[...]


def encode_kernel(slots, wanted, *refs):
    part_refs = refs[:slots]
    pad_ref, ws_ref, wr_ref, owed_ref, hidden_ref, table_ref, *out_refs = refs[slots:]
    nodes = part_refs[0].shape[0]
    owed = [owed_ref[q * wanted : (q + 1) * wanted, :] for q in range(4)]
    total = part_refs[0][...].astype(F32)
    for ref in part_refs[1:]:
        total = total + ref[...].astype(F32)
    total = total.astype(BF16)
    for m in range(hidden_ref.shape[0]):
        hidden = silu(dot(total, pad_ref[m]))
        hidden_ref[m] = hidden
        project(m, hidden, owed, ws_ref[0], wr_ref[0], table_ref, out_refs, wanted, nodes)


def pieces(chunk):
    step = chunk // 3
    return [(k, step) for k in range(0, chunk, step)]


def early_kernel(chunk, local_ref, table_ref, gather_ref, scatter_ref, sums_ref, terms_ref):
    members, depth, _ = table_ref.shape
    edges = gather_ref.shape[0]
    sums_ref[...] = jnp.zeros(sums_ref.shape, F32)

    @pl.loop(0, edges // chunk)
    def _(c):
        at = pl.multiple_of(c * chunk, chunk)
        here = c < local_ref[0] // chunk

        @pl.when(here)
        def _():
            for m in range(members):
                found = [
                    silu(dot(gather_ref[pl.ds(at + k, n), 0:depth], table_ref[m])).astype(BF16)
                    for k, n in pieces(chunk)
                ]
                sums_ref[m] += dot(scatter_ref[:, pl.ds(at, chunk)], jnp.concatenate(found, 0))

        @pl.when(jnp.logical_not(here))
        def _():
            for m in range(members):
                for k, n in pieces(chunk):
                    terms_ref[m, pl.ds(at + k, n), :] = dot(gather_ref[pl.ds(at + k, n), 0:depth], table_ref[m])


def late_messages(chunk, local_ref, gather_ref, scatter_ref, depth, terms_ref, known, chosen, sums_ref):
    edges = gather_ref.shape[0]

    @pl.loop(local_ref[0] // chunk, edges // chunk)
    def _(c):
        at = pl.multiple_of(c * chunk, chunk)
        for m in chosen:
            found = []
            for k, n in pieces(chunk):
                v = terms_ref[m, pl.ds(at + k, n), :] + dot(gather_ref[pl.ds(at + k, n), depth:], known[m])
                found.append(silu(v).astype(BF16))
            sums_ref[m] += dot(scatter_ref[:, pl.ds(at, chunk)], jnp.concatenate(found, 0))


def layer_kernel(layer, only, wanted, chunk, *refs):
    local_ref, hidden_ref, terms_ref, owed_ref, gather_ref, scatter_ref, early_ref = refs[:7]
    halo_refs, wu_ref = refs[9:11] + refs[7:9], refs[11]
    last = only is not None
    if last:
        dec_ref, out_ref, known, sums = refs[12:]
    else:
        ws_ref, wr_ref, next_hidden_ref, next_table_ref, *out_refs, known, sums = refs[12:]
    members, nodes, width = hidden_ref.shape
    chosen = (only,) if last else range(members)
    for m in chosen:
        sums[m] = early_ref[m]
        for q in range(4):
            known[m, q * wanted : (q + 1) * wanted, :] = halo_refs[q][m * wanted : (m + 1) * wanted, :]
        known[m, 4 * wanted :, :] = jnp.zeros((known.shape[1] - 4 * wanted, width), BF16)
    late_messages(chunk, local_ref, gather_ref, scatter_ref, 2 * nodes, terms_ref, known, chosen, sums)
    if not last:
        owed = [owed_ref[q * wanted : (q + 1) * wanted, :] for q in range(4)]
    for m in chosen:
        hidden = hidden_ref[m] + dot(sums[m].astype(BF16), wu_ref[layer])
        if last:
            out_ref[...] = dot(dec_ref[...], normalize(hidden), 1, 1).astype(BF16)
        else:
            next_hidden_ref[m] = hidden
            project(m, hidden, owed, ws_ref[layer + 1], wr_ref[layer + 1], next_table_ref, out_refs, wanted, nodes)


def land_kernel(rows, slots, member, u_ref, w_ref, *refs):
    corr_refs, (out_ref, tile, sem) = refs[:slots], refs[-3:]
    quantities, width = corr_refs[0].shape[0], u_ref.shape[1] // rows
    total = u_ref[member * quantities : (member + 1) * quantities, :]
    for s in range(slots):
        total = total + dot(corr_refs[s][...], w_ref[(slots - s) % slots])
    for r in range(rows):
        tile[pl.ds(r, quantities, stride=rows), :] = total[:, r * width : (r + 1) * width]
    size = quantities * rows
    copy = pltpu.make_async_copy(tile, out_ref.at[member * size : (member + 1) * size], sem)
    copy.start()
    copy.wait()


def land(kernel, x, args, onward, size, lon):
    spaces = [pl.BlockSpec(memory_space=pltpu.VMEM)] * (len(args) - onward)
    spaces += [pl.BlockSpec(memory_space=pl.ANY)] * onward
    return pl.pallas_call(
        kernel,
        out_shape=shape(x.shape, F32),
        in_specs=spaces,
        out_specs=pl.BlockSpec(memory_space=pl.ANY),
        scratch_shapes=[pltpu.VMEM((size, x.shape[1]), F32), pltpu.SemaphoreType.DMA],
        input_output_aliases={len(args) - 1: 0} if onward else {},
        compiler_params=pltpu.CompilerParams(vmem_limit_bytes=(16 + lon) * MIB),
        cost_estimate=cost(1e9, 6 * MIB),
    )(*args)


def body(
    fields, wind_east, wind_north, diffusion, inflow_owner, inflow_cell, inflow_node, inflow_weight,
    encoder, sender_weight, receiver_weight, update_weight, decoder, edge_sender, edge_receiver, halo_rows,
    outflow_owner, outflow_node, outflow_cell, outflow_weight,
):
    members, quantities, rows, width = fields.shape
    count, cells = members * quantities, rows * width
    lon, lat = lax.axis_size("lon"), lax.axis_size("lat")
    me = lax.axis_index("lon").astype(I32).reshape(1)
    lat_at = lax.axis_index("lat").astype(I32).reshape(1)
    blocks, entries = inflow_cell.shape
    hid = encoder.shape[1]
    layers = sender_weight.shape[0]
    edges = edge_sender.shape[-1]
    wanted = halo_rows.shape[-1]
    nodes = NODE_DEV
    cap = max(2, -(-2 * blocks // lon))

    def shift(v, s):
        return lax.ppermute(v, "lon", [(i, (i + s) % lon) for i in range(lon)])

    def peer(v, s):
        if lon & (lon - 1):
            return shift(v, s)
        return lax.ppermute(v, "lon", [(i, i ^ s) for i in range(lon)])

    def up(v):
        return lax.ppermute(v, "lat", [(i, (i + 1) % lat) for i in range(lat)])

    def down(v):
        return lax.ppermute(v, "lat", [((i + 1) % lat, i) for i in range(lat)])

    x = fields.reshape(count * rows, width)
    halo = halo_rows.reshape(4, wanted)
    rates = (wind_east, wind_north, diffusion)
    tall = 2 * count + 16
    tables = (inflow_node, inflow_cell, inflow_weight)
    taken = pltpu.SMEM((lon,), I32)
    to_north, to_south, side, wind, in_lists = call(
        functools.partial(edge_kernel, rows, lon),
        [shape((tall, width), BF16), shape((tall, width), BF16), shape((2, 4 * rows, count), F32),
         shape((3, rows, width), F32), shape((lon, 3 * cap, entries), F32)],
        (me, inflow_owner.reshape(blocks), x, *rates, halo, *tables),
        smem=2,
        away=8,
        scratch=[
            pltpu.VMEM(x.shape, F32),
            pltpu.VMEM(halo.shape, I32),
            pltpu.VMEM((16, width), F32),
            taken,
            *(pltpu.VMEM(v.shape, v.dtype) for v in tables),
            pltpu.SemaphoreType.DMA((8,)),
        ],
        vmem=56,
        cost=cost(0, 8 * MIB),
    )
    south, north = up(to_north), down(to_south)
    into = build(lon, nodes, cells, (in_lists,))
    side, into = lax.optimization_barrier((side, into))
    to_east, to_west = call(
        functools.partial(side_kernel, rows),
        (shape((4 * rows, count), BF16), shape((4 * rows, count), BF16)),
        (south, north, side),
        vmem=4,
        cost=cost(0, 4 * MIB),
    )
    west, east = shift(to_east, 1), shift(to_west, lon - 1)

    x, _ = lax.optimization_barrier((x, to_east))
    mid, rate = call(
        functools.partial(inner_kernel, rows, lat),
        (shape((rows + 2, count, width), F32), shape((5, rows + 2, width), F32)),
        (lat_at, x, wind, south, north),
        smem=1,
        vmem=12,
        cost=cost(1e9, 6 * MIB),
    )
    u, *parts = call(
        functools.partial(step_kernel, rows, lat, lon),
        [shape((count, cells), F32)] + [shape((nodes, count), F32)] + [shape((nodes, count), BF16)] * (lon - 1),
        (lat_at, mid, rate, side, west, east, into),
        smem=1,
        scratch=[
            pltpu.VMEM((32, count), F32),
            pltpu.VMEM((count, (rows + 2) * width), F32),
            pltpu.VMEM((count, cells), F32),
            pltpu.VMEM((rows + 2, count, width), F32),
            pltpu.VMEM((count, cells), BF16),
        ],
        vmem=14 + lon * 2,
        cost=cost(2 * lon * nodes * cells * count, 16 * MIB),
    )
    parts, edge_sender, edge_receiver, outflow_node = lax.optimization_barrier(
        (parts, edge_sender, edge_receiver, outflow_node)
    )
    parts = parts[:1] + [peer(parts[s], s) for s in range(lon - 1, 0, -1)]

    known = 2 * nodes + 256 * -(-4 * wanted // 256)
    chunk = edges // 2
    gather, scatter, local = call(
        link_kernel,
        (shape((edges, known), BF16), shape((nodes, edges), BF16), shape((1,), I32)),
        (edge_sender.reshape(1, edges), edge_receiver.reshape(1, edges)),
        small=1,
        scratch=[pltpu.VMEM((edges, edges), BF16)],
        vmem=24,
        cost=cost(2 * edges * edges * 48, 8 * MIB),
    )
    out_lists = call(
        functools.partial(sort_kernel, lon),
        [shape((3 * cap, entries), F32)] * lon,
        (me, outflow_owner.reshape(blocks), outflow_node, outflow_cell, outflow_weight),
        smem=2,
        scratch=[pltpu.VMEM((lon, 3 * cap, entries), F32), taken],
        vmem=4,
        cost=cost(0, MIB),
    )
    scatter, out_lists = lax.optimization_barrier((scatter, out_lists))
    out_lists = [out_lists[0]] + [peer(out_lists[s], s) for s in range(1, lon)]
    parts, out_lists = lax.optimization_barrier((parts, out_lists))
    onto = build(lon, nodes, cells, out_lists)

    reply = [shape((members * wanted, hid), BF16)] * 4
    state = [shape((members, nodes, hid), F32), shape((members, 2 * nodes, hid), BF16)]
    owed, pad = call(
        functools.partial(owed_kernel, rows, wanted),
        (shape((4 * wanted, nodes), BF16), shape((members, count, hid), BF16)),
        (south, north, west, east, encoder),
        vmem=8,
        cost=cost(0, 4 * MIB),
    )
    hidden, table, *out = call(
        functools.partial(encode_kernel, lon, wanted),
        state + reply,
        (*parts, pad, sender_weight, receiver_weight, owed),
        vmem=16,
        cost=cost(2e9, 8 * MIB),
    )
    for layer in range(layers):
        halos = [shift(out[3], 1), shift(out[2], lon - 1), up(out[1]), down(out[0])]
        early, terms = call(
            functools.partial(early_kernel, chunk),
            (shape((members, nodes, hid), F32), shape((members, edges, hid), F32)),
            (local, table, gather, scatter),
            smem=1,
            vmem=16,
            cost=cost(3e9, 8 * MIB),
        )
        last = layer == layers - 1
        args = (local, hidden, terms, owed, gather, scatter, early, *halos, update_weight)
        scratch = [pltpu.VMEM((members, known - 2 * nodes, hid), BF16), pltpu.VMEM((members, nodes, hid), F32)]
        if last:
            corrs = [
                call(
                    functools.partial(layer_kernel, layer, m, wanted, chunk), shape((quantities, nodes), BF16),
                    (*args, decoder.T), smem=1, scratch=scratch, vmem=20, cost=cost(2e9, 8 * MIB),
                )
                for m in range(members)
            ]
        else:
            hidden, table, *out = call(
                functools.partial(layer_kernel, layer, None, wanted, chunk),
                state + reply,
                (*args, sender_weight, receiver_weight),
                smem=1,
                scratch=scratch,
                vmem=20,
                cost=cost(4e9, 12 * MIB),
            )
    corrs = [[v] + [peer(v, s) for s in range(lon - 1, 0, -1)] for v in corrs]
    out = None
    for m in range(members):
        args = (u, onto, *corrs[m]) if out is None else (u, onto, *corrs[m], out)
        out = land(functools.partial(land_kernel, rows, lon, m), x, args, out is not None, rows * quantities, lon)
    return out.reshape(members, quantities, rows, width)


def solution(mesh):
    tile, block, part = P("lat", "lon"), P(("lat", "lon"), None), P("lat", "lon", None)
    placed = (P("member", None, "lat", "lon"), tile, tile, tile, block, block, block, block)
    placed += (P(),) * 5 + (part, part, P("lat", "lon", None, None)) + (block,) * 4
    return jax.shard_map(
        body, mesh=mesh, in_specs=placed, out_specs=P("member", None, "lat", "lon"), check_vma=False
    )
```

```python
import functools

import jax
import jax.numpy as jnp
from jax import lax
from jax.experimental import pallas as pl
from jax.experimental.pallas import tpu as pltpu
from jax.sharding import PartitionSpec as P

F32, BF16, I32 = jnp.float32, jnp.bfloat16, jnp.int32
MIB = 1 << 20
SCALE = 0.05
NODE_DEV = 256


def dot(a, b, ca=1, cb=0):
    return lax.dot_general(a, b, (((ca,), (cb,)), ((), ())), preferred_element_type=F32)


def iota(shape, dim):
    return lax.broadcasted_iota(I32, shape, dim)


def call(kernel, outs, args, smem=0, away=0, small=0, scratch=(), vmem=32, cost=None):
    single = not isinstance(outs, (list, tuple))
    spaces = [pltpu.SMEM] * smem + [pl.ANY] * away + [pltpu.VMEM] * (len(args) - smem - away)
    if single:
        out_specs = pl.BlockSpec(memory_space=pltpu.VMEM)
    else:
        homes = [pltpu.VMEM] * (len(outs) - small) + [pltpu.SMEM] * small
        out_specs = tuple(pl.BlockSpec(memory_space=m) for m in homes)
    return pl.pallas_call(
        kernel,
        out_shape=outs if single else tuple(outs),
        in_specs=[pl.BlockSpec(memory_space=m) for m in spaces],
        out_specs=out_specs,
        scratch_shapes=list(scratch),
        compiler_params=pltpu.CompilerParams(vmem_limit_bytes=vmem * MIB),
        cost_estimate=cost,
    )(*args)


def cost(flops, bytes_accessed):
    return pl.CostEstimate(flops=int(flops * SCALE), bytes_accessed=int(bytes_accessed * SCALE), transcendentals=0)


def shape(dims, dtype):
    return jax.ShapeDtypeStruct(tuple(dims), dtype)


def split(v):
    hi = v.astype(BF16).astype(F32)
    return hi, v - hi


def pick_columns(width):
    row, lane = iota((16, width), 0), iota((16, width), 1)
    hit = (row == 0) & (lane == 0) | (row == 1) & (lane == 1)
    hit = hit | (row == 2) & (lane == width - 1) | (row == 3) & (lane == width - 2)
    return hit.astype(F32).astype(BF16)


def coefficients(we, wn, d):
    pe, ne = jnp.maximum(we, 0.0), jnp.minimum(we, 0.0)
    pn, nn = jnp.maximum(wn, 0.0), jnp.minimum(wn, 0.0)
    return 1.0 - pe + ne - pn + nn - 4.0 * d, pe + d, d - ne, pn + d, d - nn


def edge_kernel(rows, slots, me_ref, lat_ref, owner_ref, *refs):
    homes, (first_ref, second_ref, side_ref, rate_ref, in_ref) = refs[:8], refs[8:13]
    x_ref, halo_ref, block, taken, *tables, sems = refs[13:]
    held = [x_ref, *(rate_ref.at[j] for j in range(3)), halo_ref, *tables]
    copies = [pltpu.make_async_copy(a, b, sems.at[k]) for k, (a, b) in enumerate(zip(homes, held))]
    for copy in copies:
        copy.start()
    for copy in copies[1:]:
        copy.wait()
    sort_blocks(slots, me_ref[0], owner_ref, tables, in_ref, taken)
    copies[0].wait()
    wanted = halo_ref.shape[1]
    count = x_ref.shape[0] // rows
    width = x_ref.shape[1]

    def row(r):
        return x_ref[pl.ds(r, count, stride=rows), :].astype(BF16)

    odd = lax.rem(lat_ref[0], 2)
    for out_ref, south in ((first_ref, odd), (second_ref, 1 - odd)):
        near, far = (1 - south) * (rows - 1), south + (1 - south) * (rows - 2)
        out_ref[0:count, :] = row(near)
        out_ref[count : 2 * count, :] = row(far)
        block[...] = jnp.zeros(block.shape, F32)
        for j in range(3):
            hi, lo = split(rate_ref[j, pl.ds(near, 1), :])
            block[j : j + 1, :] = hi
            block[j + 3 : j + 4, :] = lo
        block[6:7, 0:wanted] = halo_ref[pl.ds(1 - south, 1), :].astype(F32)
        out_ref[2 * count : 2 * count + 16, :] = block[...].astype(BF16)
    lane = iota((rows, count), 1)
    for i, (c, q) in enumerate(((width - 1, 3), (0, 2))):
        side_ref[i, 2 * rows : 3 * rows, :] = jnp.zeros((rows, count), F32)
        side_ref[i, 2 * rows + 2 : 2 * rows + 3, 0:wanted] = halo_ref[q : q + 1, :].astype(F32)
        rates = jnp.zeros((rows, count), F32)
        for j in range(3):
            hi, lo = split(rate_ref[j][:, c : c + 1])
            rates = jnp.where(lane == j, hi, jnp.where(lane == j + 3, lo, rates))
        side_ref[i, 3 * rows : 4 * rows, :] = rates
    pick = pick_columns(width)
    for r in range(rows):
        got = dot(pick, row(r), 1, 1)
        for i, k in enumerate((2, 0)):
            side_ref[i, r : r + 1, :] = got[k : k + 1, :]
            side_ref[i, rows + r : rows + r + 1, :] = got[k + 1 : k + 2, :]


def side_kernel(rows, lat_ref, first_ref, second_ref, side_ref, east_ref, west_ref, south_ref, north_ref):
    @pl.when(lax.rem(lat_ref[0], 2) == 0)
    def _():
        south_ref[...] = second_ref[...]
        north_ref[...] = first_ref[...]

    @pl.when(lax.rem(lat_ref[0], 2) == 1)
    def _():
        south_ref[...] = first_ref[...]
        north_ref[...] = second_ref[...]

    count, width = side_ref.shape[2], south_ref.shape[1]
    pick = pick_columns(width)
    south = dot(pick, south_ref[0:count, :], 1, 1)
    north = dot(pick, north_ref[0:count, :], 1, 1)
    line = iota((4 * rows, count), 0)
    for i, (out_ref, k) in enumerate(((east_ref, 2), (west_ref, 0))):
        v = jnp.where(line == 2 * rows, south[k : k + 1, :], side_ref[i])
        out_ref[...] = jnp.where(line == 2 * rows + 1, north[k : k + 1, :], v).astype(BF16)


def slot_of(owner, me, slots):
    if slots & (slots - 1):
        return lax.rem(owner - me + slots, slots)
    return lax.bitwise_xor(owner, me)


def sort_blocks(slots, me, owner_ref, lists, hold, taken):
    cap = hold.shape[1] // 3
    hold[...] = jnp.zeros(hold.shape, F32)
    for s in range(slots):
        taken[s] = 0

    @pl.loop(0, lists[0].shape[0])
    def _(b):
        s = slot_of(owner_ref[b], me, slots)
        at = jnp.minimum(taken[s], cap - 1)
        taken[s] = at + 1
        for k in range(3):
            hold[s, pl.ds(k * cap + at, 1), :] = lists[k][pl.ds(b, 1), :].astype(F32)


def sort_kernel(slots, me_ref, owner_ref, *refs):
    out_refs, (hold, taken) = refs[3 : 3 + slots], refs[3 + slots :]
    sort_blocks(slots, me_ref[0], owner_ref, refs[:3], hold, taken)
    for s in range(slots):
        out_refs[s][...] = hold[s]


def build_kernel(slots, *refs):
    list_refs, (out_ref, hot, spread) = refs[:-3], refs[-3:]
    nodes, cells = out_ref.shape[1], out_ref.shape[2]
    if len(list_refs) < slots:
        list_refs = [list_refs[0].at[s] for s in range(slots)]
    cap, entries = list_refs[0].shape[0] // 3, list_refs[0].shape[1]
    node_ids = iota((nodes, entries), 0).astype(F32)
    cell_ids = iota((entries, cells), 1).astype(F32)
    for s in range(slots):
        ref = list_refs[s]
        columns = ref[...].T
        for c in range(cap):
            lanes = slice(c * entries, (c + 1) * entries)
            cell, weight = (columns[:, k * cap + c : k * cap + c + 1] for k in (1, 2))
            hot[:, lanes] = jnp.where(node_ids == ref[c : c + 1, :], 1.0, 0.0).astype(BF16)
            spread[lanes, :] = jnp.where(cell_ids == cell, weight, 0.0).astype(BF16)
        out_ref[s] = dot(hot[...], spread[...]).astype(BF16)


def build(slots, nodes, cells, lists):
    cap, entries = lists[0].shape[-2] // 3, lists[0].shape[-1]
    size = slots * nodes * cells
    return call(
        functools.partial(build_kernel, slots),
        shape((slots, nodes, cells), BF16),
        lists,
        scratch=[pltpu.VMEM((nodes, cap * entries), BF16), pltpu.VMEM((cap * entries, cells), BF16)],
        vmem=8 + 3 * size // MIB,
        cost=cost(2 * size * cap * entries, 4 * size),
    )


def mend(rows, lat, lat_ref, c0, cw, ce, cs, cn):
    line = iota(c0.shape, 0)
    ps = jnp.where((line == 0) & (lat_ref[0] == 0), 1.0, 0.0)
    pn = jnp.where((line == rows - 1) & (lat_ref[0] == lat - 1), 1.0, 0.0)
    return c0 + ps * cs + pn * cn, cw, ce, cs * (1.0 - ps), cn * (1.0 - pn)


def turning(width):
    k, col = iota((2 * width, 2 * width), 0), iota((2 * width, 2 * width), 1)
    k = jnp.where(k < width, k, k - width)
    return jnp.where(jnp.where(col < width, col - 1, col - width + 1) == k, 1.0, 0.0).astype(BF16)


def advance(turn, rates, v, below, above):
    width = v.shape[1]
    hi = v.astype(BF16)
    turned = dot(jnp.concatenate([hi, (v - hi.astype(F32)).astype(BF16)], 1), turn)
    c0, cw, ce, cs, cn = rates
    return c0 * v + cw * turned[:, 0:width] + ce * turned[:, width : 2 * width] + cs * below + cn * above


def inner_kernel(rows, lat, lat_ref, x_ref, wind_ref, south_ref, north_ref, mid_ref, rate):
    count, width = mid_ref.shape[1], x_ref.shape[1]
    own = mend(rows, lat, lat_ref, *coefficients(wind_ref[0], wind_ref[1], wind_ref[2]))
    outer = []
    for ref in (south_ref, north_ref):
        v = ref[2 * count : 2 * count + 16, :].astype(F32)
        outer.append(coefficients(*(v[j : j + 1, :] + v[j + 3 : j + 4, :] for j in range(3))))
    for j in range(5):
        rate[j, 0:1, :] = outer[0][j]
        rate[j, 1 : rows + 1, :] = own[j]
        rate[j, rows + 1 : rows + 2, :] = outer[1][j]
    turn = turning(width)

    def cell_row(r):
        if r < 0:
            return south_ref[(-1 - r) * count : -r * count, :].astype(F32)
        if r >= rows:
            return north_ref[(r - rows) * count : (r - rows + 1) * count, :].astype(F32)
        return x_ref[pl.ds(r, count, stride=rows), :]

    for r in range(-1, rows + 1):
        rates = [rate[j, r + 1 : r + 2, :] for j in range(5)]
        mid_ref[r + 1] = advance(turn, rates, cell_row(r), cell_row(r - 1), cell_row(r + 1))


def step_kernel(rows, lat, slots, lat_ref, mid_ref, rate, side_ref, west_ref, east_ref, a_ref, u_ref, *rest):
    part_refs, (ring, b1, b2, mid, flat) = rest[:slots], rest[slots:]
    count, width = side_ref.shape[2], mid_ref.shape[2]
    west, east = west_ref[...].astype(F32), east_ref[...].astype(F32)
    w1, w2, w_corner, w_rate = (west[k * rows : (k + 1) * rows, :] for k in range(4))
    e1, e2, e_corner, e_rate = (east[k * rows : (k + 1) * rows, :] for k in range(4))
    half = ring.shape[0] // 2

    def place(out_ref, lines):
        k, col = iota((2 * half, lines * width), 0), iota((2 * half, lines * width), 1)
        hit = jnp.where(k < half, k * width, (k - half) * width + width - 1) == col
        out_ref[...] = dot(ring[...].astype(BF16), jnp.where(hit, 1.0, 0.0).astype(BF16), 0, 0)

    ring[...] = jnp.zeros(ring.shape, F32)
    for base, corner, near, j, c in ((0, w_corner, w1, 1, 0), (half, e_corner, e1, 2, width - 1)):
        k = rate[j, :, c : c + 1]
        ring[base : base + 1, :] = k[0:1, :] * corner[0:1, :]
        ring[base + 1 : base + 1 + rows, :] = k[1 : rows + 1, :] * near
        ring[base + 1 + rows : base + 2 + rows, :] = k[rows + 1 : rows + 2, :] * corner[1:2, :]
    place(b1, rows + 2)

    def ring_col(rates, corner, v, out_w, out_e):
        rates = coefficients(*(rates[:, j : j + 1] + rates[:, j + 3 : j + 4] for j in range(3)))
        k0, kw, ke, ks, kn = mend(rows, lat, lat_ref, *rates)
        line = iota(v.shape, 0)
        to_s = jnp.where(line == 0, corner[0:1, :], pltpu.roll(v, 1, 0))
        to_n = jnp.where(line == rows - 1, corner[1:2, :], pltpu.roll(v, rows - 1, 0))
        return k0 * v + kw * out_w + ke * out_e + ks * to_s + kn * to_n

    ring[...] = jnp.zeros(ring.shape, F32)
    kw, ke = rate[1, 1 : rows + 1, 0:1], rate[2, 1 : rows + 1, width - 1 : width]
    ring[0:rows, :] = kw * ring_col(w_rate, w_corner, w1, w2, side_ref[1, 0:rows, :])
    ring[half : half + rows, :] = ke * ring_col(e_rate, e_corner, e1, side_ref[0, 0:rows, :], e2)
    place(b2, rows)

    for r in range(rows + 2):
        mid[r] = mid_ref[r] + b1[:, r * width : (r + 1) * width]
    turn = turning(width)
    for r in range(rows):
        here = slice(r * width, (r + 1) * width)
        rates = [rate[j, r + 1 : r + 2, :] for j in range(5)]
        new = advance(turn, rates, mid[r + 1], mid[r], mid[r + 2]) + b2[:, here]
        u_ref[:, here] = new
        flat[:, here] = new.astype(BF16)
    for s in range(slots):
        part_refs[s][...] = dot(a_ref[s], flat[...], 1, 1).astype(part_refs[s].dtype)


def silu_of_half(h):
    return h + h * jnp.tanh(h)


def normalize(v):
    return (v * lax.rsqrt(jnp.mean(v * v, axis=-1, keepdims=True) + 1e-06)).astype(BF16)


def link_kernel(sender_ref, receiver_ref, gather_ref, scatter_ref, local_ref, order):
    edges, known = gather_ref.shape
    nodes = scatter_ref.shape[0]
    sender, receiver = sender_ref[...], receiver_ref[...]
    local = jnp.where(sender < nodes, 1.0, 0.0)
    order[...] = jnp.where(iota((edges, edges), 0) < iota((edges, edges), 1), 1.0, 0.0).astype(BF16)
    before = dot(jnp.broadcast_to(local, (16, edges)).astype(BF16), order[...])[0:1, :]
    total = jnp.sum(local)
    local_ref[0] = total.astype(I32)
    index = iota((1, edges), 1).astype(F32)
    place = jnp.where(sender < nodes, before, total + index - before)
    order[...] = jnp.where(iota((edges, edges), 0).astype(F32) == place, 1.0, 0.0).astype(BF16)
    line = iota((16, edges), 0)
    high = sender // nodes
    keys = jnp.where(line == 0, sender - high * nodes, jnp.where(line == 1, high, jnp.where(line == 2, receiver, 0)))
    keys = keys.astype(F32).astype(BF16)
    cols = dot(order[...], keys, 1, 1)
    sender, receiver = cols[:, 0:1] + nodes * cols[:, 1:2], cols[:, 2:3]
    lane = iota((edges, nodes), 1).astype(F32)
    gather_ref[:, 0:nodes] = jnp.where(sender == lane, 0.5, 0.0).astype(BF16)
    gather_ref[:, nodes : 2 * nodes] = jnp.where(receiver == lane, 0.5, 0.0).astype(BF16)
    rest = (iota((edges, known - 2 * nodes), 1) + nodes).astype(F32)
    gather_ref[:, 2 * nodes :] = jnp.where(sender == rest, 0.5, 0.0).astype(BF16)
    row = dot(keys, order[...], 1, 1)[2:3, :]
    scatter_ref[...] = jnp.where(row == iota((nodes, edges), 0).astype(F32), 1.0, 0.0).astype(BF16)


def project(m, hidden, owed, ws, wr, table_ref, out_refs, wanted, nodes):
    normed = normalize(hidden)
    source = dot(normed, ws).astype(BF16)
    table_ref[m, 0:nodes, :] = source
    table_ref[m, nodes : 2 * nodes, :] = dot(normed, wr).astype(BF16)
    for q in range(4):
        out_refs[q][m * wanted : (m + 1) * wanted, :] = dot(owed[q], source).astype(BF16)


def owed_kernel(rows, wanted, south_ref, north_ref, west_ref, east_ref, enc_ref, owed_ref, pad_ref):
    nodes = owed_ref.shape[1]
    count = west_ref.shape[1]
    lists = [ref[2 * count : 2 * count + 16, :].astype(F32)[6:7, :] for ref in (south_ref, north_ref)]
    lists += [ref[2 * rows : 4 * rows, 0:128].astype(F32)[2:3, :] for ref in (west_ref, east_ref)]
    for q in range(4):
        hot = jnp.where(iota((nodes, 128), 0).astype(F32) == lists[q], 1.0, 0.0)
        owed_ref[q * wanted : (q + 1) * wanted, :] = hot.T[0:wanted, :].astype(BF16)
    quantities = enc_ref.shape[0]
    pad_ref[...] = jnp.zeros(pad_ref.shape, BF16)
    for m in range(pad_ref.shape[0]):
        pad_ref[m, m * quantities : (m + 1) * quantities, :] = enc_ref[...]


def encode_kernel(slots, wanted, *refs):
    part_refs = refs[:slots]
    pad_ref, ws_ref, wr_ref, owed_ref, hidden_ref, table_ref, *out_refs = refs[slots:]
    nodes = part_refs[0].shape[0]
    owed = [owed_ref[q * wanted : (q + 1) * wanted, :] for q in range(4)]
    total = part_refs[0][...].astype(F32)
    for ref in part_refs[1:]:
        total = total + ref[...].astype(F32)
    total = total.astype(BF16)
    for m in range(hidden_ref.shape[0]):
        hidden = silu_of_half(0.5 * dot(total, pad_ref[m]))
        hidden_ref[m] = hidden
        project(m, hidden, owed, ws_ref[0], wr_ref[0], table_ref, out_refs, wanted, nodes)


def pieces(chunk):
    step = chunk // 3
    return [(k, step) for k in range(0, chunk, step)]


def early_kernel(chunk, local_ref, table_ref, gather_ref, scatter_ref, sums_ref, terms_ref):
    members, depth, _ = table_ref.shape
    edges = gather_ref.shape[0]
    sums_ref[...] = jnp.zeros(sums_ref.shape, F32)

    @pl.loop(0, edges // chunk)
    def _(c):
        at = pl.multiple_of(c * chunk, chunk)
        here = c < local_ref[0] // chunk

        @pl.when(here)
        def _():
            for m in range(members):
                found = [
                    silu_of_half(dot(gather_ref[pl.ds(at + k, n), 0:depth], table_ref[m])).astype(BF16)
                    for k, n in pieces(chunk)
                ]
                sums_ref[m] += dot(scatter_ref[:, pl.ds(at, chunk)], jnp.concatenate(found, 0))

        @pl.when(jnp.logical_not(here))
        def _():
            for m in range(members):
                for k, n in pieces(chunk):
                    terms_ref[m, pl.ds(at + k, n), :] = dot(gather_ref[pl.ds(at + k, n), 0:depth], table_ref[m])


def late_messages(chunk, local_ref, gather_ref, scatter_ref, depth, terms_ref, known, chosen, sums_ref):
    edges = gather_ref.shape[0]

    @pl.loop(local_ref[0] // chunk, edges // chunk)
    def _(c):
        at = pl.multiple_of(c * chunk, chunk)
        for m in chosen:
            found = []
            for k, n in pieces(chunk):
                v = terms_ref[m, pl.ds(at + k, n), :] + dot(gather_ref[pl.ds(at + k, n), depth:], known[m])
                found.append(silu_of_half(v).astype(BF16))
            sums_ref[m] += dot(scatter_ref[:, pl.ds(at, chunk)], jnp.concatenate(found, 0))


def layer_kernel(layer, only, wanted, chunk, *refs):
    local_ref, hidden_ref, terms_ref, owed_ref, gather_ref, scatter_ref, early_ref = refs[:7]
    halo_refs, wu_ref = refs[9:11] + refs[7:9], refs[11]
    last = only is not None
    if last:
        dec_ref, out_ref, known, sums = refs[12:]
    else:
        ws_ref, wr_ref, next_hidden_ref, next_table_ref, *out_refs, known, sums = refs[12:]
    members, nodes, width = hidden_ref.shape
    chosen = (only,) if last else range(members)
    for m in chosen:
        sums[m] = early_ref[m]
        for q in range(4):
            known[m, q * wanted : (q + 1) * wanted, :] = halo_refs[q][m * wanted : (m + 1) * wanted, :]
        known[m, 4 * wanted :, :] = jnp.zeros((known.shape[1] - 4 * wanted, width), BF16)
    late_messages(chunk, local_ref, gather_ref, scatter_ref, 2 * nodes, terms_ref, known, chosen, sums)
    if not last:
        owed = [owed_ref[q * wanted : (q + 1) * wanted, :] for q in range(4)]
    for m in chosen:
        hidden = hidden_ref[m] + dot(sums[m].astype(BF16), wu_ref[layer])
        if last:
            out_ref[...] = dot(dec_ref[...], normalize(hidden), 1, 1).astype(BF16)
        else:
            next_hidden_ref[m] = hidden
            project(m, hidden, owed, ws_ref[layer + 1], wr_ref[layer + 1], next_table_ref, out_refs, wanted, nodes)


def land_kernel(rows, slots, member, u_ref, w_ref, *refs):
    corr_refs, (out_ref, tile, sem) = refs[:slots], refs[-3:]
    quantities, width = corr_refs[0].shape[0], u_ref.shape[1] // rows
    total = u_ref[member * quantities : (member + 1) * quantities, :]
    for s in range(slots):
        total = total + dot(corr_refs[s][...], w_ref[(slots - s) % slots])
    for r in range(rows):
        tile[pl.ds(r, quantities, stride=rows), :] = total[:, r * width : (r + 1) * width]
    size = quantities * rows
    copy = pltpu.make_async_copy(tile, out_ref.at[member * size : (member + 1) * size], sem)
    copy.start()
    copy.wait()


def land(kernel, x, args, onward, size, lon):
    spaces = [pl.BlockSpec(memory_space=pltpu.VMEM)] * (len(args) - onward)
    spaces += [pl.BlockSpec(memory_space=pl.ANY)] * onward
    return pl.pallas_call(
        kernel,
        out_shape=shape(x.shape, F32),
        in_specs=spaces,
        out_specs=pl.BlockSpec(memory_space=pl.ANY),
        scratch_shapes=[pltpu.VMEM((size, x.shape[1]), F32), pltpu.SemaphoreType.DMA],
        input_output_aliases={len(args) - 1: 0} if onward else {},
        compiler_params=pltpu.CompilerParams(vmem_limit_bytes=(16 + lon) * MIB),
        cost_estimate=cost(1e9, 6 * MIB),
    )(*args)


def body(
    fields, wind_east, wind_north, diffusion, inflow_owner, inflow_cell, inflow_node, inflow_weight,
    encoder, sender_weight, receiver_weight, update_weight, decoder, edge_sender, edge_receiver, halo_rows,
    outflow_owner, outflow_node, outflow_cell, outflow_weight,
):
    members, quantities, rows, width = fields.shape
    count, cells = members * quantities, rows * width
    lon, lat = lax.axis_size("lon"), lax.axis_size("lat")
    me = lax.axis_index("lon").astype(I32).reshape(1)
    lat_at = lax.axis_index("lat").astype(I32).reshape(1)
    blocks, entries = inflow_cell.shape
    hid = encoder.shape[1]
    layers = sender_weight.shape[0]
    edges = edge_sender.shape[-1]
    wanted = halo_rows.shape[-1]
    nodes = NODE_DEV
    cap = max(2, -(-2 * blocks // lon))

    def shift(v, s):
        return lax.ppermute(v, "lon", [(i, (i + s) % lon) for i in range(lon)])

    def peer(v, s):
        if lon & (lon - 1):
            return shift(v, s)
        return lax.ppermute(v, "lon", [(i, i ^ s) for i in range(lon)])

    def up(v):
        return lax.ppermute(v, "lat", [(i, (i + 1) % lat) for i in range(lat)])

    def down(v):
        return lax.ppermute(v, "lat", [((i + 1) % lat, i) for i in range(lat)])

    x = fields.reshape(count * rows, width)
    halo = halo_rows.reshape(4, wanted)
    rates = (wind_east, wind_north, diffusion)
    tall = 2 * count + 16
    tables = (inflow_node, inflow_cell, inflow_weight)
    taken = pltpu.SMEM((lon,), I32)
    first, second, side, wind, in_lists = call(
        functools.partial(edge_kernel, rows, lon),
        [shape((tall, width), BF16), shape((tall, width), BF16), shape((2, 4 * rows, count), F32),
         shape((3, rows, width), F32), shape((lon, 3 * cap, entries), F32)],
        (me, lat_at, inflow_owner.reshape(blocks), x, *rates, halo, *tables),
        smem=3,
        away=8,
        scratch=[
            pltpu.VMEM(x.shape, F32),
            pltpu.VMEM(halo.shape, I32),
            pltpu.VMEM((16, width), F32),
            taken,
            *(pltpu.VMEM(v.shape, v.dtype) for v in tables),
            pltpu.SemaphoreType.DMA((8,)),
        ],
        vmem=56,
        cost=cost(0, 8 * MIB),
    )
    first, second = (
        lax.ppermute(v, "lat", [(i, j if 0 <= (j := ((i - k) ^ 1) + k) < lat else i) for i in range(lat)])
        for k, v in enumerate((first, second))
    )
    into = build(lon, nodes, cells, (in_lists,))
    side, into = lax.optimization_barrier((side, into))
    to_east, to_west, south, north = call(
        functools.partial(side_kernel, rows),
        [shape((4 * rows, count), BF16)] * 2 + [shape((tall, width), BF16)] * 2,
        (lat_at, first, second, side),
        smem=1,
        vmem=4,
        cost=cost(0, 4 * MIB),
    )
    west, east = shift(to_east, 1), shift(to_west, lon - 1)

    x, _ = lax.optimization_barrier((x, to_east))
    mid, rate = call(
        functools.partial(inner_kernel, rows, lat),
        (shape((rows + 2, count, width), F32), shape((5, rows + 2, width), F32)),
        (lat_at, x, wind, south, north),
        smem=1,
        vmem=12,
        cost=cost(1e9, 6 * MIB),
    )
    u, *parts = call(
        functools.partial(step_kernel, rows, lat, lon),
        [shape((count, cells), F32)] + [shape((nodes, count), F32)] + [shape((nodes, count), BF16)] * (lon - 1),
        (lat_at, mid, rate, side, west, east, into),
        smem=1,
        scratch=[
            pltpu.VMEM((32, count), F32),
            pltpu.VMEM((count, (rows + 2) * width), F32),
            pltpu.VMEM((count, cells), F32),
            pltpu.VMEM((rows + 2, count, width), F32),
            pltpu.VMEM((count, cells), BF16),
        ],
        vmem=14 + lon * 2,
        cost=cost(2 * lon * nodes * cells * count, 16 * MIB),
    )
    parts, edge_sender, edge_receiver, outflow_node = lax.optimization_barrier(
        (parts, edge_sender, edge_receiver, outflow_node)
    )
    parts = parts[:1] + [peer(parts[s], s) for s in range(lon - 1, 0, -1)]

    known = 2 * nodes + 256 * -(-4 * wanted // 256)
    chunk = edges // 2
    gather, scatter, local = call(
        link_kernel,
        (shape((edges, known), BF16), shape((nodes, edges), BF16), shape((1,), I32)),
        (edge_sender.reshape(1, edges), edge_receiver.reshape(1, edges)),
        small=1,
        scratch=[pltpu.VMEM((edges, edges), BF16)],
        vmem=24,
        cost=cost(2 * edges * edges * 48, 8 * MIB),
    )
    out_lists = call(
        functools.partial(sort_kernel, lon),
        [shape((3 * cap, entries), F32)] * lon,
        (me, outflow_owner.reshape(blocks), outflow_node, outflow_cell, outflow_weight),
        smem=2,
        scratch=[pltpu.VMEM((lon, 3 * cap, entries), F32), taken],
        vmem=4,
        cost=cost(0, MIB),
    )
    scatter, out_lists = lax.optimization_barrier((scatter, out_lists))
    out_lists = [out_lists[0]] + [peer(out_lists[s], s) for s in range(1, lon)]
    parts, out_lists = lax.optimization_barrier((parts, out_lists))
    onto = build(lon, nodes, cells, out_lists)

    reply = [shape((members * wanted, hid), BF16)] * 4
    state = [shape((members, nodes, hid), F32), shape((members, 2 * nodes, hid), BF16)]
    owed, pad = call(
        functools.partial(owed_kernel, rows, wanted),
        (shape((4 * wanted, nodes), BF16), shape((members, count, hid), BF16)),
        (south, north, west, east, encoder),
        vmem=8,
        cost=cost(0, 4 * MIB),
    )
    hidden, table, *out = call(
        functools.partial(encode_kernel, lon, wanted),
        state + reply,
        (*parts, pad, sender_weight, receiver_weight, owed),
        vmem=16,
        cost=cost(2e9, 8 * MIB),
    )
    for layer in range(layers):
        halos = [shift(out[3], 1), shift(out[2], lon - 1), up(out[1]), down(out[0])]
        early, terms = call(
            functools.partial(early_kernel, chunk),
            (shape((members, nodes, hid), F32), shape((members, edges, hid), F32)),
            (local, table, gather, scatter),
            smem=1,
            vmem=16,
            cost=cost(3e9, 8 * MIB),
        )
        last = layer == layers - 1
        args = (local, hidden, terms, owed, gather, scatter, early, *halos, update_weight)
        scratch = [pltpu.VMEM((members, known - 2 * nodes, hid), BF16), pltpu.VMEM((members, nodes, hid), F32)]
        if last:
            corrs = [
                call(
                    functools.partial(layer_kernel, layer, m, wanted, chunk), shape((quantities, nodes), BF16),
                    (*args, decoder.T), smem=1, scratch=scratch, vmem=20, cost=cost(2e9, 8 * MIB),
                )
                for m in range(members)
            ]
        else:
            hidden, table, *out = call(
                functools.partial(layer_kernel, layer, None, wanted, chunk),
                state + reply,
                (*args, sender_weight, receiver_weight),
                smem=1,
                scratch=scratch,
                vmem=20,
                cost=cost(4e9, 12 * MIB),
            )
    corrs = [[v] + [peer(v, s) for s in range(lon - 1, 0, -1)] for v in corrs]
    out = None
    for m in range(members):
        args = (u, onto, *corrs[m]) if out is None else (u, onto, *corrs[m], out)
        out = land(functools.partial(land_kernel, rows, lon, m), x, args, out is not None, rows * quantities, lon)
    return out.reshape(members, quantities, rows, width)


def solution(mesh):
    tile, block, part = P("lat", "lon"), P(("lat", "lon"), None), P("lat", "lon", None)
    placed = (P("member", None, "lat", "lon"), tile, tile, tile, block, block, block, block)
    placed += (P(),) * 5 + (part, part, P("lat", "lon", None, None)) + (block,) * 4
    return jax.shard_map(
        body, mesh=mesh, in_specs=placed, out_specs=P("member", None, "lat", "lon"), check_vma=False
    )
```
